256 devices in a mesh: expert: 32 (over x, z), vocab: 8 (over y, core).
Axes of the slice: x: 4, y: 4, z: 8, core: 2. Of those that a mesh axis runs over, the one named last changes fastest.
Arguments:
- tokens: bfloat16 [512, 7168], P(('expert', 'vocab')), may hold values from -6 to 6
- routes: int32 [512, 8], P(('expert', 'vocab')), may hold values from 0 to 31, all different within a row; in each aligned block of 16 rows (0 to 15, 16 to 31, ...) at most 8 rows name the same one
- route_gates: bfloat16 [512, 8], P(('expert', 'vocab')), may hold values from 0.049804688 to 0.59765625
- expert_gate: bfloat16 [32, 7168, 1536], P('expert', None, 'vocab'), may hold values from -0.0625 to 0.0625
- expert_up: bfloat16 [32, 7168, 1536], P('expert', None, 'vocab'), may hold values from -0.0625 to 0.0625
- expert_down: bfloat16 [32, 1536, 7168], P('expert', 'vocab'), may hold values from -0.15625 to 0.15625
- norm_gain: float32 [7168], replicated, may hold values from 0.25 to 1.75
- head_weight: bfloat16 [7168, 65536], P(None, ('expert', 'vocab')), may hold values from -17.008401 to 17.008401
- targets: int32 [512], P(('expert', 'vocab')), may hold values from 0 to 65535
Outputs:
- logprob: float32 [512], P(('expert', 'vocab'))
- hidden: bfloat16 [512, 7168], P(('expert', 'vocab'))
The draws below stay inside these ranges and needn't reach their ends.
Inputs may be any that keep to these rules, and one draw needn't show every extreme that they name: `routes`: each row names 8 different experts. In each aligned block of 16 rows no expert is named by more than 8 rows, and in every draw some expert is named by exactly 8 rows of some block.
All inputs are finite; a program needn't handle non-finite values.
Results may differ from the reference program's by a relative error of at most 0.017.
Values may be sent and summed in bfloat16 or wider, within the bound.
No kernel may reach another device: no remote copies, remote signals or barrier semaphores. Data moves between devices by JAX's collectives and lax.ppermute only.
A program may use at most 128 MiB of HBM per device.

```python
import math
import jax
import jax.numpy as jnp
import numpy as np
from jax import lax

D = 7168
FF = 1536
VOCAB = 65536
TOP = 8
EXPERTS = 32
GROUP = 16
TOKENS = 512
MOST = 8
N_VOCAB = 8


def draw_head_weight(key, part):
    key = jax.random.fold_in(key, 7)
    base_key = jax.random.fold_in(key, 0)
    values = jnp.clip(jax.random.normal(base_key, (D, VOCAB), jnp.float32), -6.0, 6.0) * (3.0 / math.sqrt(D))
    return values.astype(jnp.bfloat16)


def plant(values, rng, smallest, high):
    longest = values.shape.index(max(values.shape))
    spots = []
    for shift in (0, 1):
        where = [jax.random.randint(jax.random.fold_in(rng, axis), (), 0, length) for axis, length in enumerate(values.shape)]
        where[longest] = (where[longest] + shift) % values.shape[longest]
        spots.append(tuple(where))
    return values.at[spots[0]].set(smallest).at[spots[1]].set(high)


def levels(rng, dims, cuts, least, top_value):
    gain = 1.0
    for axis_at, shards_of in cuts:
        heights = jax.random.uniform(jax.random.fold_in(jax.random.fold_in(rng, 6), axis_at), (shards_of,), jnp.float32, least / len(cuts), top_value / len(cuts))
        gain = gain * jnp.repeat(jnp.exp(heights), dims[axis_at] // shards_of).reshape((-1,) + (1,) * (len(dims) - 1 - axis_at))
    return gain


def routed_block(stream_key, own, number, rows, number_of, top, most, skew):
    order = jax.random.permutation(stream_key, number_of)
    heavy_load, common = shares(number_of, rows * top, most, skew, True), shares(number_of, rows * top, most, skew, False)
    places = jnp.arange(number_of)

    def named(tallies, offset_by):
        used = int((tallies > 0).sum())
        fixed = max(1, used // 4)
        shifted = fixed + (places - fixed + offset_by * (used - fixed)) % max(1, number_of - fixed)
        return jnp.zeros((number_of,), jnp.int32).at[order[jnp.where(places < fixed, places, shifted)]].set(jnp.asarray(tallies, jnp.int32))

    tallies = jnp.where(number % 4 == 0, named(heavy_load, number // 4), named(common, number - number // 4 - 1))
    mixed = jax.random.permutation(jax.random.fold_in(own, 3), number_of)
    giver, receiver = mixed[0:number_of // 2 * 2:2], mixed[1:number_of // 2 * 2:2]
    slack = jnp.minimum(tallies[giver] - 1, most - tallies[receiver]) // 2
    slack = jnp.where((giver == order[0]) | (receiver == order[0]) | (tallies[receiver] == 0), 0, jnp.maximum(slack, 0))
    shifted = jax.random.randint(jax.random.fold_in(own, 4), (number_of // 2,), 0, 1 << 20) % (slack + 1)
    tallies = tallies.at[giver].add(-shifted).at[receiver].add(shifted)
    members = jnp.searchsorted(jnp.cumsum(tallies), jnp.arange(rows * top), side="right").astype(jnp.int32)
    table = members.reshape(top, rows).T
    table = table[jax.random.permutation(jax.random.fold_in(own, 1), rows)]
    offset_by = jax.random.randint(jax.random.fold_in(own, 2), (rows, 1), 0, top)
    return jnp.take_along_axis(table, (jnp.arange(top)[None, :] + offset_by) % top, axis=1)


def shares(amount, total, most, slope, full):
    loads = [(1 << 20) // math.isqrt(grade ** slope) + 1 for grade in range(1, amount + 1)]
    largest = most if full else min(most, max(-(-total // amount), total * loads[0] // sum(loads)))
    least = 1 if total - largest >= amount - 1 else 0
    given, surplus = [largest] + [least] * (amount - 1), total - largest - least * (amount - 1)
    while surplus > 0:
        candidates = [i for i in range(1, amount) if given[i] < largest] or [i for i in range(1, amount) if given[i] < most]
        mass, budget = sum([loads[i] for i in candidates]), surplus
        for i in candidates:
            more = min(most - given[i], max(1, budget * loads[i] // mass), surplus)
            given[i] = given[i] + more
            surplus = surplus - more
    return np.array(given)


def gaussian(rng, dims, width, reach, cuts=(), held_as=jnp.bfloat16):
    drawn = jax.random.normal(rng, dims, jnp.float32) * width
    if len(cuts) > 0:
        drawn = levels(rng, dims, cuts, -0.22, 0.18) * drawn
    return jnp.clip(drawn, min=-reach, max=reach).astype(held_as)


def setup_inputs(seed: int = 0) -> dict:
    key_list = jax.random.split(jax.random.key(seed), 10)
    tokens = gaussian(key_list[0], (TOKENS, D), 1.0, 6.0, ((0, 256),))
    routes_keys = jax.random.split(jax.random.fold_in(key_list[1], 1), TOKENS // GROUP)
    routes_turns = jax.random.permutation(jax.random.fold_in(key_list[1], 3), TOKENS // GROUP)
    routes = jax.vmap(lambda own, number: routed_block(jax.random.fold_in(key_list[1], 2), own, number, GROUP, EXPERTS, TOP, MOST, 2))(routes_keys, routes_turns).reshape((TOKENS, TOP))
    route_gates = jnp.clip(0.049804688 + 0.54785156 * jax.random.uniform(key_list[2], (TOKENS, TOP), jnp.float32) ** levels(key_list[2], (TOKENS, TOP), ((0, 256),), -0.2, 0.2), 0.049804688, 0.59765625).astype(jnp.bfloat16)
    expert_gate = gaussian(key_list[3], (EXPERTS, D, FF), D ** -0.5, 0.0625, ((0, 32), (2, 8)))
    expert_up = gaussian(key_list[4], (EXPERTS, D, FF), D ** -0.5, 0.0625, ((0, 32), (2, 8)))
    expert_down = gaussian(key_list[5], (EXPERTS, FF, D), FF ** -0.5, 0.15625, ((0, 32), (1, 8)))
    norm_gain = jnp.clip(1.0 + 0.15 * jax.random.normal(key_list[6], (D,), jnp.float32), 0.25, 1.75)
    head_weight = draw_head_weight(jax.random.fold_in(key_list[9], 71), 0)
    targets = plant(jax.random.randint(key_list[8], (TOKENS,), 0, VOCAB), jax.random.fold_in(key_list[8], 1), 0, VOCAB - 1).astype(jnp.int32)
    return dict(tokens=tokens, routes=routes, route_gates=route_gates, expert_gate=expert_gate, expert_up=expert_up, expert_down=expert_down, norm_gain=norm_gain, head_weight=head_weight, targets=targets)


def slot_numbers(route_block, expert_count):
    flat_routes = route_block.reshape(-1)
    onehot = (flat_routes[:, None] == jnp.arange(expert_count, dtype=jnp.int32)[None, :]).astype(jnp.int32)
    occurrence = jnp.cumsum(onehot, axis=0) - 1
    return lax.optimization_barrier(jnp.sum(onehot * occurrence, axis=1)).reshape(route_block.shape)

def expert_apply(operands):
    slot_rows, gate_matrix, up_matrix, down_matrix = operands
    gate_part = jnp.dot(slot_rows, gate_matrix, preferred_element_type=jnp.float32)
    up_part = jnp.dot(slot_rows, up_matrix, preferred_element_type=jnp.float32)
    active = (jax.nn.silu(gate_part) * up_part).astype(jnp.bfloat16)
    range_size = FF // N_VOCAB
    summed = jnp.zeros((slot_rows.shape[0], D), jnp.float32)
    for share in range(N_VOCAB):
        piece_act = active[:, share * range_size:(share + 1) * range_size]
        piece_down = down_matrix[share * range_size:(share + 1) * range_size]
        rounded = jnp.dot(piece_act, piece_down, preferred_element_type=jnp.float32).astype(jnp.bfloat16)
        rounded = lax.optimization_barrier(rounded)
        summed = summed + rounded.astype(jnp.float32)
    return summed

def reference(tokens, routes, route_gates, expert_gate, expert_up, expert_down, norm_gain, head_weight, targets):
    block_count = TOKENS // GROUP
    slot_number = jax.vmap(lambda block: slot_numbers(block, EXPERTS))(routes.reshape(block_count, GROUP, TOP))
    slot_number = slot_number.reshape(TOKENS, TOP)
    block_index = (jnp.arange(TOKENS, dtype=jnp.int32) // GROUP)[:, None]
    row_index = (block_index * MOST + slot_number).astype(jnp.int32)
    spread_rows = jnp.broadcast_to(tokens[:, None, :], (TOKENS, TOP, D))
    buffers = jnp.zeros((EXPERTS, block_count * MOST, D), tokens.dtype).at[routes, row_index].set(spread_rows)
    outputs = lax.map(expert_apply, (buffers, expert_gate, expert_up, expert_down))
    chosen = outputs[routes, row_index]
    moe = lax.optimization_barrier(jnp.sum(chosen * route_gates.astype(jnp.float32)[:, :, None], axis=1))
    hidden = (tokens.astype(jnp.float32) + moe).astype(jnp.bfloat16)
    widened = hidden.astype(jnp.float32)
    inverse = lax.rsqrt(lax.optimization_barrier(jnp.mean(widened * widened, axis=-1, keepdims=True)) + 1e-06)
    normed = (widened * inverse * norm_gain).astype(jnp.bfloat16)
    logits = jnp.dot(normed, head_weight, preferred_element_type=jnp.float32)
    row_top = lax.optimization_barrier(jnp.max(logits, axis=1))
    log_norm = row_top + jnp.log(lax.optimization_barrier(jnp.sum(jnp.exp(logits - row_top[:, None]), axis=1)))
    target_logit = jnp.take_along_axis(logits, targets[:, None].astype(jnp.int32), axis=1)[:, 0]
    return (target_logit - log_norm, hidden)
```

```python
import jax
import jax.numpy as jnp
from jax import lax
from jax.sharding import Mesh, PartitionSpec as P

META = 128
PLANE = ("x", "y", "c")


def on_plane(value, step):
    nx, ny = lax.axis_size("x"), lax.axis_size("y")
    pairs = []
    for x in range(nx):
        for y in range(ny):
            for c in range(2):
                tx, ty = ((x + step) % nx, y) if c == 0 else (x, (y + step) % ny)
                pairs.append(((x * ny + y) * 2 + c, (tx * ny + ty) * 2 + c))
    return lax.ppermute(value, PLANE, pairs)


def on_other(value, step):
    nx, ny = lax.axis_size("x"), lax.axis_size("y")
    pairs = []
    for x in range(nx):
        for y in range(ny):
            for c in range(2):
                tx, ty = ((x + step) % nx, y) if c == 1 else (x, (y + step) % ny)
                pairs.append(((x * ny + y) * 2 + c, (tx * ny + ty) * 2 + c))
    return lax.ppermute(value, PLANE, pairs)


def swap(value):
    return lax.ppermute(value, "c", [(0, 1), (1, 0)])


def gather_rows(block):
    depth, width = lax.axis_size("z"), block.shape[1]
    spread = jnp.broadcast_to(block[None], (depth,) + block.shape)
    column = lax.all_to_all(spread, "z", 0, 0, tiled=True)
    column = column.reshape(depth, 2, 2, width).transpose(1, 0, 2, 3).reshape(4 * depth, width)
    wide = jnp.concatenate(
        [column, on_plane(column, 1), on_plane(column, -1), on_plane(column, 2)], axis=0
    )
    half = wide.shape[0] // 2
    top, low = wide[:half], wide[half:]
    up_top, down_low = on_other(top, 1), on_other(low, -1)
    up_low, down_top = on_other(low, 1), on_other(top, -1)
    far_top, far_low = on_other(up_top, 1), on_other(down_low, -1)
    return jnp.concatenate([wide, up_top, up_low, down_top, down_low, far_top, far_low], axis=0)


def add(*values):
    total = values[0].astype(jnp.float32)
    for value in values[1:]:
        total = total + value.astype(jnp.float32)
    return total


def scatter_rows(partial):
    depth, width = lax.axis_size("z"), partial.shape[1]
    rows = partial.shape[0] // 8
    own = partial[: 2 * rows]
    up_top, up_low, down_top, down_low, far_top, far_low = (
        partial[i * rows : (i + 1) * rows] for i in range(2, 8)
    )
    via_top, via_low = on_other(far_top, -1), on_other(far_low, 1)
    back_low, fore_top = on_other(up_low, -1), on_other(down_top, 1)
    back_top = on_other(add(up_top, via_top).astype(jnp.bfloat16), -1)
    fore_low = on_other(add(down_low, via_low).astype(jnp.bfloat16), 1)
    wide = jnp.concatenate(
        [add(own[:rows], back_top, fore_top), add(own[rows:], back_low, fore_low)], axis=0
    ).astype(jnp.bfloat16)
    quarter = wide.shape[0] // 4
    column = add(
        wide[:quarter],
        on_plane(wide[quarter : 2 * quarter], -1),
        on_plane(wide[2 * quarter : 3 * quarter], 1),
        on_plane(wide[3 * quarter :], 2),
    ).astype(jnp.bfloat16)
    column = column.reshape(2, depth, 2, width).transpose(1, 0, 2, 3).reshape(depth, 4, width)
    arrived = lax.all_to_all(column, "z", 0, 0, tiled=True)
    return jnp.sum(arrived.astype(jnp.float32), axis=0)


def reorder(value):
    rows, width = value.shape
    cut = value.reshape(4, 4, 2, rows // 32, width)
    return jnp.flip(cut.swapaxes(0, 1), axis=2).reshape(rows, width)


def shards(
    tokens,
    routes,
    route_gates,
    expert_gate,
    expert_up,
    expert_down,
    norm_gain,
    head_weight,
    targets,
):
    first = lax.axis_index("c") == 0
    core = lax.axis_index("c")
    width = tokens.shape[1]
    half = width // 2
    mine, others = core * half, (1 - core) * half

    def cut(value, start, dim):
        return lax.dynamic_slice_in_dim(value, start, half, dim)

    def in_order(own, other, axis):
        return jnp.concatenate(
            [jnp.where(first, own, other), jnp.where(first, other, own)], axis=axis
        )

    meta = jnp.concatenate(
        [
            routes.astype(jnp.bfloat16),
            route_gates,
            (targets // 256).astype(jnp.bfloat16)[:, None],
            (targets % 256).astype(jnp.bfloat16)[:, None],
        ],
        axis=1,
    )
    meta = jnp.pad(meta, ((0, 0), (0, META - meta.shape[1])))
    keep = jnp.concatenate([cut(tokens, mine, 1), meta], axis=1)
    give = jnp.concatenate([cut(tokens, others, 1), meta], axis=1)
    chip_rows = jnp.concatenate([keep, swap(give)], axis=0)

    gate_rows, up_rows = expert_gate[0], expert_up[0]
    gate_weight = in_order(cut(gate_rows, mine, 0), swap(cut(gate_rows, others, 0)), 1)
    up_weight = in_order(cut(up_rows, mine, 0), swap(cut(up_rows, others, 0)), 1)
    down_weight = in_order(
        cut(expert_down[0], mine, 1), swap(cut(expert_down[0], others, 1)), 0
    )
    head = in_order(cut(head_weight, mine, 0), swap(cut(head_weight, others, 0)), 1)
    gain = lax.dynamic_slice_in_dim(norm_gain, mine, half, 0)
    in_weight = jnp.concatenate([gate_weight, up_weight], axis=1)

    all_rows = gather_rows(chip_rows)
    meta = all_rows[:, half:].astype(jnp.float32)
    my_expert = lax.axis_index(("x", "z")).astype(jnp.float32)
    weight = jnp.sum(jnp.where(meta[:, :8] == my_expert, meta[:, 8:16], 0.0), axis=1)
    goals = meta[:, 16].astype(jnp.int32) * 256 + meta[:, 17].astype(jnp.int32)

    inner = jnp.dot(all_rows[:, :half], in_weight, preferred_element_type=jnp.float32)
    inner = inner + reorder(swap(inner))
    hidden_units = inner.shape[1] // 2
    active = jax.nn.silu(inner[:, :hidden_units]) * inner[:, hidden_units:]
    active = (active * weight[:, None]).astype(jnp.bfloat16)
    partial = jnp.dot(active, down_weight, preferred_element_type=jnp.float32).astype(jnp.bfloat16)
    moe = scatter_rows(partial)

    hidden = (chip_rows[:, :half].astype(jnp.float32) + moe).astype(jnp.bfloat16)
    other_half = swap(hidden[2:])
    hidden_out = in_order(hidden[:2], other_half, 1)
    widened = hidden.astype(jnp.float32)
    squares = jnp.sum(widened * widened, axis=1, keepdims=True)
    high = lax.reduce_precision(squares, 8, 7)
    middle = lax.reduce_precision(squares - high, 8, 7)
    low = squares - high - middle
    pieces = jnp.concatenate([high, middle, low], axis=1).astype(jnp.bfloat16)
    scaled = jnp.concatenate(
        [
            (widened * gain).astype(jnp.bfloat16),
            jnp.pad(pieces, ((0, 0), (0, META - 3))),
        ],
        axis=1,
    )

    every_row = gather_rows(scaled)
    logits = jnp.dot(every_row[:, :half], head, preferred_element_type=jnp.float32)
    row_squares = jnp.sum(every_row[:, half : half + 3].astype(jnp.float32), axis=1, keepdims=True)
    both = jnp.concatenate(
        [logits, jnp.broadcast_to(row_squares, (row_squares.shape[0], META))], axis=1
    )
    count, columns = both.shape
    both = both.reshape(4, 4, 2, count // 32, columns)
    received = swap(both[:, :, 1])
    both = (both[:, :, 0] + received.swapaxes(0, 1)).reshape(count // 2, columns)
    goals = goals.reshape(16, 2, count // 32)[:, 0].reshape(count // 2)

    vocab = columns - META
    inverse = lax.rsqrt(both[:, vocab:vocab + 1] / width + 1e-06)
    logits = both[:, :vocab] * inverse
    chip = lax.axis_index(("x", "z", "y"))
    matches = jnp.arange(vocab, dtype=jnp.int32)[None, :] + chip * vocab == goals[:, None]
    picked = jnp.sum(jnp.where(matches, logits, 0.0), axis=1)
    top = jnp.max(logits, axis=1)
    total = jnp.sum(jnp.exp(logits - top[:, None]), axis=1)

    steps = jnp.array([0, -1, 1, 2], jnp.int32)
    here_x, here_y = lax.axis_index("x"), lax.axis_index("y")
    depth = lax.axis_size("z")
    outer, inner_step = steps[:, None], steps[None, :]
    from_x = (here_x + jnp.where(first, inner_step, outer)) % lax.axis_size("x")
    from_y = (here_y + jnp.where(first, outer, inner_step)) % lax.axis_size("y")
    base = (from_x * depth * lax.axis_size("y") + from_y).reshape(16, 1, 1)
    place = (base + jnp.arange(depth, dtype=jnp.int32)[None, :, None] * lax.axis_size("y")) * 2
    place = (place + jnp.arange(2, dtype=jnp.int32)[None, None, :]).reshape(count // 2)
    onehot = place[None, :] == jnp.arange(count // 2, dtype=jnp.int32)[:, None]
    stats = jnp.stack(
        [jnp.sum(jnp.where(onehot, s[None, :], 0.0), axis=1) for s in (top, total, picked)], axis=1
    )
    stats = stats.reshape(count // 4, 6)
    arrived = lax.all_to_all(stats, ("x", "z", "y"), 0, 0, tiled=True)
    arrived = arrived.reshape(count // 4, 2, 3)
    row_top = jnp.max(arrived[:, :, 0], axis=0)
    exp_total = jnp.sum(arrived[:, :, 1] * jnp.exp(arrived[:, :, 0] - row_top), axis=0)
    logprob = jnp.sum(arrived[:, :, 2], axis=0) - (row_top + jnp.log(exp_total))
    return (logprob, hidden_out)


def solution(mesh):
    fine = Mesh(mesh.devices.reshape(4, 8, 4, 2), ("x", "z", "y", "c"))
    rows = ("x", "z", "y", "c")
    in_specs = (
        P(rows, None),
        P(rows, None),
        P(rows, None),
        P(("x", "z"), None, ("y", "c")),
        P(("x", "z"), None, ("y", "c")),
        P(("x", "z"), ("y", "c"), None),
        P(),
        P(None, rows),
        P(rows),
    )
    out_specs = (P(rows), P(rows, None))
    return jax.shard_map(shards, mesh=fine, in_specs=in_specs, out_specs=out_specs, check_vma=False)
```

```python
import jax
import jax.numpy as jnp
from jax import lax
from jax.experimental import pallas as pl
from jax.experimental.pallas import tpu as pltpu
from jax.sharding import Mesh, PartitionSpec as P

META = 128
PLANE = ("x", "y", "c")
SMEM = pl.BlockSpec(memory_space=pltpu.SMEM)
VMEM = pl.BlockSpec(memory_space=pltpu.VMEM)


def move(value, step, along):
    nx, ny = lax.axis_size("x"), lax.axis_size("y")
    pairs = []
    for x in range(nx):
        for y in range(ny):
            for c in range(2):
                tx, ty = ((x + step) % nx, y) if c == along else (x, (y + step) % ny)
                pairs.append(((x * ny + y) * 2 + c, (tx * ny + ty) * 2 + c))
    return lax.ppermute(value, PLANE, pairs)


def swap(value):
    return lax.ppermute(value, "c", [(0, 1), (1, 0)])


def add(*values):
    total = values[0].astype(jnp.float32)
    for value in values[1:]:
        total = total + value.astype(jnp.float32)
    return total


def together(*values):
    return lax.optimization_barrier(values)


def column_rows(spread):
    depth, rows, width = spread.shape
    return lax.all_to_all(spread, "z", 0, 0, tiled=True).reshape(depth * rows, width)


def first_axis_rows(column):
    return jnp.concatenate(
        [column, move(column, 1, 0), move(column, -1, 0), move(column, 2, 0)], axis=0
    )


def second_axis_rows(wide, *extra):
    half = wide.shape[0] // 2
    top, low = wide[:half], wide[half:]
    up_top, down_low, *extra = together(move(top, 1, 1), move(low, -1, 1), *extra)
    up_low, down_top = move(low, 1, 1), move(top, -1, 1)
    far_top, far_low = move(up_top, 1, 1), move(down_low, -1, 1)
    rows = jnp.concatenate([wide, up_top, up_low, down_top, down_low, far_top, far_low], axis=0)
    return rows, *extra


def narrow(*values):
    return add(*values).astype(jnp.bfloat16)


def fold_second_axis(partial):
    rows = partial.shape[0] // 8
    own_top, own_low, up_top, up_low, down_top, down_low, far_top, far_low = (
        partial[i * rows : (i + 1) * rows] for i in range(8)
    )
    via_top, via_low = together(move(far_top, -1, 1), move(far_low, 1, 1))
    back_low, fore_top = move(up_low, -1, 1), move(down_top, 1, 1)
    back_top, fore_low = together(narrow(up_top, via_top), narrow(down_low, via_low))
    back_top, fore_low = move(back_top, -1, 1), move(fore_low, 1, 1)
    return jnp.concatenate(
        [narrow(own_top, back_top, fore_top), narrow(own_low, back_low, fore_low)], axis=0
    )


def fold_first_axis(partial):
    rows = partial.shape[0] // 4
    own, up, down, far = (partial[i * rows : (i + 1) * rows] for i in range(4))
    return narrow(own, move(up, -1, 0), move(down, 1, 0), move(far, 2, 0))


def fold_column(partial):
    depth, width = lax.axis_size("z"), partial.shape[1]
    arrived = lax.all_to_all(partial.reshape(depth, 2, width), "z", 0, 0, tiled=True)
    return jnp.sum(arrived.astype(jnp.float32), axis=0)


def spread_kernel(target_ref, token_ref, route_ref, gate_ref, out_ref):
    depth, rows, width = out_ref.shape
    lane = lax.broadcasted_iota(jnp.int32, (rows, META), 1)
    row = lax.broadcasted_iota(jnp.int32, (rows, META), 0)
    routes = route_ref[...].astype(jnp.float32)
    gates = gate_ref[...].astype(jnp.float32)
    meta = jnp.zeros((rows, META), jnp.float32)
    for index in range(routes.shape[1]):
        meta = jnp.where(lane == index, routes[:, index : index + 1], meta)
        meta = jnp.where(lane == 8 + index, gates[:, index : index + 1], meta)
    goal = jnp.where(row == 0, target_ref[0], target_ref[1])
    meta = jnp.where(lane == 16, (goal >> 8).astype(jnp.float32), meta)
    meta = jnp.where(lane == 17, (goal & 255).astype(jnp.float32), meta)
    meta = meta.astype(jnp.bfloat16)
    for index in range(depth):
        out_ref[index, :, : width - META] = token_ref[...]
        out_ref[index, :, width - META :] = meta


def spread_tokens(tokens, routes, route_gates, targets, depth):
    rows, width = tokens.shape
    return pl.pallas_call(
        spread_kernel,
        out_shape=jax.ShapeDtypeStruct((depth, rows, width + META), tokens.dtype),
        in_specs=[SMEM, VMEM, VMEM, VMEM],
        out_specs=VMEM,
        name="spread",
    )(targets, tokens, routes, route_gates)


def stats_kernel(place_ref, own_ref, other_ref, goal_ref, out_ref, stats):
    rows = own_ref.shape[0]
    lane = lax.broadcasted_iota(jnp.int32, (rows, META), 1)
    goal = goal_ref[...]
    own, other = own_ref[...], other_ref[...]
    top = jnp.maximum(jnp.max(own, axis=1, keepdims=True), jnp.max(other, axis=1, keepdims=True))
    total = jnp.zeros_like(top)
    picked = jnp.zeros_like(top)
    for which, value in enumerate((own, other)):
        total += jnp.sum(jnp.exp(value - top), axis=1, keepdims=True)
        column = lax.broadcasted_iota(jnp.int32, value.shape, 1) + place_ref[which]
        picked += jnp.sum(jnp.where(column == goal, value, 0.0), axis=1, keepdims=True)
    stats[...] = jnp.where(lane == 0, top, jnp.where(lane == 1, total, picked))
    block = rows // 16
    for index in range(16):
        target = pl.multiple_of(place_ref[2 + index] * block, block)
        out_ref[pl.ds(target, block), :] = stats[pl.ds(index * block, block), :]


def row_stats(own, other, goals, place):
    rows = own.shape[0]
    return pl.pallas_call(
        stats_kernel,
        out_shape=jax.ShapeDtypeStruct((rows, META), jnp.float32),
        in_specs=[SMEM, VMEM, VMEM, VMEM],
        out_specs=VMEM,
        scratch_shapes=[pltpu.VMEM((rows, META), jnp.float32)],
        compiler_params=pltpu.CompilerParams(vmem_limit_bytes=8 * 2**20),
        name="row_stats",
    )(place, own, other, goals)


def shards(
    tokens,
    routes,
    route_gates,
    expert_gate,
    expert_up,
    expert_down,
    norm_gain,
    head_weight,
    targets,
):
    width, depth = tokens.shape[1], lax.axis_size("z")

    def product(left, right):
        return jnp.dot(left, right, preferred_element_type=jnp.float32)

    column, gate, up = together(
        column_rows(spread_tokens(tokens, routes, route_gates, targets, depth)),
        swap(expert_gate),
        swap(expert_up),
    )
    rows, down = second_axis_rows(first_axis_rows(column), swap(expert_down))
    out_weight = jnp.concatenate([expert_down[0], down[0]], axis=0)
    meta = rows[:, width:].astype(jnp.float32)
    expert = lax.axis_index(("x", "z")).astype(jnp.float32)
    share = jnp.sum(jnp.where(meta[:, :8] == expert, meta[:, 8:16], 0.0), axis=1, keepdims=True)
    goals = (meta[:, 16:17] * 256.0 + meta[:, 17:18]).astype(jnp.int32)
    rows = rows[:, :width]
    inner = together(*(product(rows, w[0]) for w in (expert_gate, expert_up, gate, up)))
    active = jnp.concatenate(
        [jax.nn.silu(inner[i]) * inner[i + 1] * share for i in (0, 2)], axis=1
    )
    partial = product(together(active.astype(jnp.bfloat16))[0], out_weight)
    partial, head_weight = together(partial.astype(jnp.bfloat16), head_weight)
    folded, head = together(fold_second_axis(partial), swap(head_weight))
    heads = [head_weight, head]
    moe = fold_column(fold_first_axis(folded))

    hidden = (tokens.astype(jnp.float32) + moe).astype(jnp.bfloat16)
    widened = hidden.astype(jnp.float32)
    inverse = lax.rsqrt(jnp.mean(widened * widened, axis=-1, keepdims=True) + 1e-06)
    normed = (widened * inverse * norm_gain).astype(jnp.bfloat16)

    columns = head_weight.shape[1]
    core = lax.axis_index("c")
    chip = lax.axis_index(("x", "z", "y"))
    first = core == 0
    steps = jnp.array([0, -1, 1, 2], jnp.int32)
    outer, inner = steps[:, None], steps[None, :]
    from_x = (lax.axis_index("x") + jnp.where(first, inner, outer)) % lax.axis_size("x")
    from_y = (lax.axis_index("y") + jnp.where(first, outer, inner)) % lax.axis_size("y")
    place = jnp.concatenate(
        [
            ((chip * 2 + core) * columns)[None],
            ((chip * 2 + 1 - core) * columns)[None],
            (from_x * lax.axis_size("y") + from_y).reshape(16),
        ]
    ).astype(jnp.int32)
    column = column_rows(jnp.broadcast_to(normed[None], (depth,) + normed.shape))
    every, = second_axis_rows(first_axis_rows(column))
    logits = [product(every, head) for head in heads]
    stats = row_stats(*logits, jnp.broadcast_to(goals, (goals.shape[0], 1)), place)
    chips = lax.axis_size(("x", "y", "z"))
    stats = stats.reshape(chips, 2, META)
    arrived = lax.all_to_all(stats, ("x", "y", "z"), 0, 0, tiled=True)
    row_top = jnp.max(arrived[:, :, 0], axis=0)
    exp_total = jnp.sum(arrived[:, :, 1] * jnp.exp(arrived[:, :, 0] - row_top), axis=0)
    logprob = jnp.sum(arrived[:, :, 2], axis=0) - (row_top + jnp.log(exp_total))
    return (logprob, hidden)


def solution(mesh):
    fine = Mesh(mesh.devices.reshape(4, 8, 4, 2), ("x", "z", "y", "c"))
    rows = ("x", "z", "y", "c")
    in_specs = (
        P(rows, None),
        P(rows, None),
        P(rows, None),
        P(("x", "z"), None, ("y", "c")),
        P(("x", "z"), None, ("y", "c")),
        P(("x", "z"), ("y", "c"), None),
        P(),
        P(None, rows),
        P(rows),
    )
    out_specs = (P(rows), P(rows, None))
    return jax.shard_map(shards, mesh=fine, in_specs=in_specs, out_specs=out_specs, check_vma=False)
```

```python
import jax
import jax.numpy as jnp
from jax import lax
from jax.experimental import pallas as pl
from jax.experimental.pallas import tpu as pltpu
from jax.sharding import Mesh, PartitionSpec as P

META = 128
PLANE = ("x", "y", "c")
ANY = pl.BlockSpec(memory_space=pl.ANY)
SMEM = pl.BlockSpec(memory_space=pltpu.SMEM)
VMEM = pl.BlockSpec(memory_space=pltpu.VMEM)


def move(value, step, along):
    nx, ny = lax.axis_size("x"), lax.axis_size("y")
    pairs = []
    for x in range(nx):
        for y in range(ny):
            for c in range(2):
                tx, ty = ((x + step) % nx, y) if c == along else (x, (y + step) % ny)
                pairs.append(((x * ny + y) * 2 + c, (tx * ny + ty) * 2 + c))
    return lax.ppermute(value, PLANE, pairs)


def swap(value):
    return lax.ppermute(value, "c", [(0, 1), (1, 0)])


def add(*values):
    total = values[0].astype(jnp.float32)
    for value in values[1:]:
        total = total + value.astype(jnp.float32)
    return total


def together(*values):
    return lax.optimization_barrier(values)


def column_rows(spread):
    depth, rows, width = spread.shape
    return lax.all_to_all(spread, "z", 0, 0, tiled=True).reshape(depth * rows, width)


def first_axis_rows(column, *extra):
    up, down = move(column, 1, 0), move(column, -1, 0)
    far, *extra = together(move(column, 2, 0), *extra)
    return jnp.concatenate([column, up, down, far], axis=0), *extra


def second_axis_rows(wide, staged, *extra):
    half = wide.shape[0] // 2
    top, low = wide[:half], wide[half:]
    up_top, down_low = move(top, 1, 1), move(low, -1, 1)
    top, low, staged = together(top, low, staged)
    up_low, down_top = move(low, 1, 1), move(top, -1, 1)
    up_top, down_low, *extra = together(up_top, down_low, *extra)
    far_top, far_low = move(up_top, 1, 1), move(down_low, -1, 1)
    rows = jnp.concatenate([wide, up_top, up_low, down_top, down_low, far_top, far_low], axis=0)
    return rows, staged, *extra


def narrow(*values):
    return add(*values).astype(jnp.bfloat16)


def fold_second_axis(partial):
    rows = partial.shape[0] // 8
    own_top, own_low, up_top, up_low, down_top, down_low, far_top, far_low = (
        partial[i * rows : (i + 1) * rows] for i in range(8)
    )
    via_top, via_low = together(move(far_top, -1, 1), move(far_low, 1, 1))
    back_low, fore_top = move(up_low, -1, 1), move(down_top, 1, 1)
    back_top, fore_low = together(narrow(up_top, via_top), narrow(down_low, via_low))
    back_top, fore_low = move(back_top, -1, 1), move(fore_low, 1, 1)
    return jnp.concatenate(
        [narrow(own_top, back_top, fore_top), narrow(own_low, back_low, fore_low)], axis=0
    )


def fold_first_axis(partial):
    rows = partial.shape[0] // 4
    own, up, down, far = (partial[i * rows : (i + 1) * rows] for i in range(4))
    return narrow(own, move(up, -1, 0), move(down, 1, 0), move(far, 2, 0))


def fold_column(partial):
    depth, width = lax.axis_size("z"), partial.shape[1]
    arrived = lax.all_to_all(partial.reshape(depth, 2, width), "z", 0, 0, tiled=True)
    return jnp.sum(arrived.astype(jnp.float32), axis=0)


def spread_kernel(target_ref, token_ref, route_ref, gate_ref, out_ref):
    depth, rows, width = out_ref.shape
    lane = lax.broadcasted_iota(jnp.int32, (rows, META), 1)
    row = lax.broadcasted_iota(jnp.int32, (rows, META), 0)
    routes = route_ref[...].astype(jnp.float32)
    gates = gate_ref[...].astype(jnp.float32)
    meta = jnp.zeros((rows, META), jnp.float32)
    for index in range(routes.shape[1]):
        meta = jnp.where(lane == index, routes[:, index : index + 1], meta)
        meta = jnp.where(lane == 8 + index, gates[:, index : index + 1], meta)
    goal = jnp.where(row == 0, target_ref[0], target_ref[1])
    meta = jnp.where(lane == 16, (goal >> 8).astype(jnp.float32), meta)
    meta = jnp.where(lane == 17, (goal & 255).astype(jnp.float32), meta)
    meta = meta.astype(jnp.bfloat16)
    for index in range(depth):
        out_ref[index, :, : width - META] = token_ref[...]
        out_ref[index, :, width - META :] = meta


def spread_tokens(tokens, routes, route_gates, targets, depth):
    rows, width = tokens.shape
    return pl.pallas_call(
        spread_kernel,
        out_shape=jax.ShapeDtypeStruct((depth, rows, width + META), tokens.dtype),
        in_specs=[SMEM, VMEM, VMEM, VMEM],
        out_specs=VMEM,
        name="spread",
    )(targets, tokens, routes, route_gates)


def stage_kernel(*refs):
    sources, out, sems = refs[:-2], refs[-2], refs[-1]
    rows = sources[0].shape[0]
    copies = [
        pltpu.make_async_copy(source, out.at[pl.ds(index * rows, rows)], sems.at[index])
        for index, source in enumerate(sources)
    ]
    for copy in copies:
        copy.start()
    for copy in copies:
        copy.wait()


def stage(*weights):
    rows, width = weights[0].shape
    shape = (len(weights) * rows, width)
    return pl.pallas_call(
        stage_kernel,
        out_shape=pltpu.VMEM(shape, weights[0].dtype),
        in_specs=[ANY] * len(weights),
        out_specs=VMEM,
        scratch_shapes=[pltpu.SemaphoreType.DMA((len(weights),))],
        cost_estimate=pl.CostEstimate(
            flops=0, bytes_accessed=4 * shape[0] * shape[1], transcendentals=0
        ),
        compiler_params=pltpu.CompilerParams(vmem_limit_bytes=2**20),
        name="stage",
    )(*weights)


def expert_kernel(expert_ref, row_ref, in_ref, down_ref, out_ref, meta_ref, inner, active):
    width, units = down_ref.shape[1], down_ref.shape[0]
    part = 128 * 3
    for start in range(0, 2 * units, part):
        inner[:, start : start + part] = lax.dot_general(
            row_ref[:, :width],
            in_ref[start : start + part, :],
            (((1,), (1,)), ((), ())),
            preferred_element_type=jnp.float32,
        )
    meta = row_ref[:, width:].astype(jnp.float32)
    meta_ref[...] = meta
    lane = lax.broadcasted_iota(jnp.int32, meta.shape, 1)
    gates = pltpu.roll(meta, META - 8, 1)
    chosen = (lane < 8) & (meta == expert_ref[0].astype(jnp.float32))
    share = jnp.sum(jnp.where(chosen, gates, 0.0), axis=1, keepdims=True)
    gate = inner[:, :units]
    value = gate / (1.0 + jnp.exp(-gate)) * inner[:, units:] * share
    active[...] = value.astype(jnp.bfloat16)
    step = width // 7

    @pl.loop(0, 7)
    def _(index):
        span = pl.ds(pl.multiple_of(index * step, step), step)
        out_ref[:, span] = jnp.dot(
            active[...], down_ref[:, span], preferred_element_type=jnp.float32
        ).astype(jnp.bfloat16)


def expert_layer(rows, in_weight, out_weight, expert):
    count = rows.shape[0]
    units, width = out_weight.shape
    return pl.pallas_call(
        expert_kernel,
        out_shape=[
            jax.ShapeDtypeStruct((count, width), jnp.bfloat16),
            jax.ShapeDtypeStruct((count, META), jnp.float32),
        ],
        in_specs=[SMEM, VMEM, VMEM, VMEM],
        out_specs=[VMEM, VMEM],
        scratch_shapes=[
            pltpu.VMEM((count, 2 * units), jnp.float32),
            pltpu.VMEM((count, units), jnp.bfloat16),
        ],
        cost_estimate=pl.CostEstimate(
            flops=6 * count * units * width,
            bytes_accessed=2 * (3 * units * width + 2 * count * width),
            transcendentals=count * units,
        ),
        compiler_params=pltpu.CompilerParams(vmem_limit_bytes=16 * 2**20),
        name="expert",
    )(expert, rows, in_weight, out_weight)


def stats_kernel(place_ref, own_ref, other_ref, meta_ref, out_ref, stats):
    rows = own_ref.shape[0]
    lane = lax.broadcasted_iota(jnp.int32, (rows, META), 1)
    meta = meta_ref[...]
    goal = jnp.where(lane == 16, meta * 256.0, jnp.where(lane == 17, meta, 0.0))
    goal = jnp.sum(goal, axis=1, keepdims=True).astype(jnp.int32)
    own, other = own_ref[...], other_ref[...]
    top = jnp.maximum(jnp.max(own, axis=1, keepdims=True), jnp.max(other, axis=1, keepdims=True))
    total = jnp.zeros_like(top)
    picked = jnp.zeros_like(top)
    for which, value in enumerate((own, other)):
        total += jnp.sum(jnp.exp(value - top), axis=1, keepdims=True)
        column = lax.broadcasted_iota(jnp.int32, value.shape, 1) + place_ref[which]
        picked += jnp.sum(jnp.where(column == goal, value, 0.0), axis=1, keepdims=True)
    values = jnp.where(lane == 0, top, jnp.where(lane == 1, total, picked))
    stats[...] = jnp.where(lane < 3, values, 0.0)
    block = rows // 32
    for index in range(16):
        first = stats[pl.ds(index * 2 * block, block, 2), :]
        second = stats[pl.ds(index * 2 * block + 1, block, 2), :]
        target = pl.multiple_of(place_ref[2 + index] * block, block)
        out_ref[pl.ds(target, block), :] = first + pltpu.roll(second, 4, 1)


def combine_kernel(stats_ref, out_ref):
    stats = stats_ref[...]
    lane = lax.broadcasted_iota(jnp.int32, (1, META), 1)
    top = jnp.max(stats, axis=0, keepdims=True)
    scale = jnp.exp(stats - top)
    total = jnp.sum(pltpu.roll(scale, 1, 1) * stats, axis=0, keepdims=True)
    picked = jnp.sum(stats, axis=0, keepdims=True)
    result = pltpu.roll(picked, META - 2, 1) - top - jnp.log(pltpu.roll(total, META - 1, 1))
    out_ref[...] = jnp.where((lane == 0) | (lane == 4), result, 0.0)


def combine(stats):
    return pl.pallas_call(
        combine_kernel,
        out_shape=jax.ShapeDtypeStruct((1, META), jnp.float32),
        in_specs=[VMEM],
        out_specs=VMEM,
        compiler_params=pltpu.CompilerParams(vmem_limit_bytes=4 * 2**20),
        name="combine",
    )(stats)


def row_stats(own, other, meta, place):
    rows = own.shape[0]
    return pl.pallas_call(
        stats_kernel,
        out_shape=jax.ShapeDtypeStruct((rows // 2, META), jnp.float32),
        in_specs=[SMEM, VMEM, VMEM, VMEM],
        out_specs=VMEM,
        scratch_shapes=[pltpu.VMEM((rows, META), jnp.float32)],
        compiler_params=pltpu.CompilerParams(vmem_limit_bytes=8 * 2**20),
        name="row_stats",
    )(place, own, other, meta)


def shards(
    tokens,
    routes,
    route_gates,
    expert_gate,
    expert_up,
    expert_down,
    norm_gain,
    head_weight,
    targets,
):
    width, depth = tokens.shape[1], lax.axis_size("z")

    def product(left, right):
        return jnp.dot(left, right, preferred_element_type=jnp.float32)

    columns = head_weight.shape[1]
    core = lax.axis_index("c")
    chip = lax.axis_index(("x", "z", "y"))
    first = core == 0
    steps = jnp.array([0, -1, 1, 2], jnp.int32)
    outer, inner = steps[:, None], steps[None, :]
    from_x = (lax.axis_index("x") + jnp.where(first, inner, outer)) % lax.axis_size("x")
    from_y = (lax.axis_index("y") + jnp.where(first, outer, inner)) % lax.axis_size("y")
    place = jnp.concatenate(
        [
            ((chip * 2 + core) * columns)[None],
            ((chip * 2 + 1 - core) * columns)[None],
            (from_x * lax.axis_size("y") + from_y).reshape(16),
        ]
    ).astype(jnp.int32)
    expert = lax.axis_index(("x", "z")).astype(jnp.int32)[None]
    column, gate, up, place, expert = together(
        column_rows(spread_tokens(tokens, routes, route_gates, targets, depth)),
        swap(expert_gate),
        swap(expert_up),
        place,
        expert,
    )
    wide, down = first_axis_rows(column, swap(expert_down))
    rows, out_weight, gate, up, head = second_axis_rows(
        wide, stage(expert_down[0], down[0]), gate, up, swap(head_weight)
    )
    in_weight = stage(expert_gate[0].T, gate[0].T, expert_up[0].T, up[0].T)
    partial, meta = expert_layer(rows, in_weight, out_weight, expert)
    folded = fold_second_axis(partial)
    moe = fold_column(fold_first_axis(folded))

    hidden = (tokens.astype(jnp.float32) + moe).astype(jnp.bfloat16)
    widened = hidden.astype(jnp.float32)
    inverse = lax.rsqrt(jnp.mean(widened * widened, axis=-1, keepdims=True) + 1e-06)
    normed = (widened * inverse * norm_gain).astype(jnp.bfloat16)

    column = column_rows(jnp.broadcast_to(normed[None], (depth,) + normed.shape))
    wide, head = first_axis_rows(column, head)
    every, head = second_axis_rows(wide, stage(head))
    stats = row_stats(product(every, head_weight), product(every, head), meta, place)
    arrived = lax.all_to_all(stats, ("x", "y", "z"), 0, 0, tiled=True)
    logprob = combine(arrived)[0, 0:8:4]
    return (logprob, hidden)


def solution(mesh):
    fine = Mesh(mesh.devices.reshape(4, 8, 4, 2), ("x", "z", "y", "c"))
    rows = ("x", "z", "y", "c")
    in_specs = (
        P(rows, None),
        P(rows, None),
        P(rows, None),
        P(("x", "z"), None, ("y", "c")),
        P(("x", "z"), None, ("y", "c")),
        P(("x", "z"), ("y", "c"), None),
        P(),
        P(None, rows),
        P(rows),
    )
    out_specs = (P(rows), P(rows, None))
    return jax.shard_map(shards, mesh=fine, in_specs=in_specs, out_specs=out_specs, check_vma=False)
```

```python
import jax
import jax.numpy as jnp
from jax import lax
from jax.experimental import pallas as pl
from jax.experimental.pallas import tpu as pltpu
from jax.sharding import Mesh, PartitionSpec as P

META = 128
PLANE = ("x", "y", "c")
ANY = pl.BlockSpec(memory_space=pl.ANY)
SMEM = pl.BlockSpec(memory_space=pltpu.SMEM)
VMEM = pl.BlockSpec(memory_space=pltpu.VMEM)


def move(value, step, along):
    nx, ny = lax.axis_size("x"), lax.axis_size("y")
    pairs = []
    for x in range(nx):
        for y in range(ny):
            for c in range(2):
                tx, ty = ((x + step) % nx, y) if c == along else (x, (y + step) % ny)
                pairs.append(((x * ny + y) * 2 + c, (tx * ny + ty) * 2 + c))
    return lax.ppermute(value, PLANE, pairs)


def swap(value):
    return lax.ppermute(value, "c", [(0, 1), (1, 0)])


def add(*values):
    total = values[0].astype(jnp.float32)
    for value in values[1:]:
        total = total + value.astype(jnp.float32)
    return total


def together(*values):
    return lax.optimization_barrier(values)


def column_rows(spread):
    depth, rows, width = spread.shape
    return lax.all_to_all(spread, "z", 0, 0, tiled=True).reshape(depth * rows, width)


def first_axis_rows(column, *extra):
    up, down = move(column, 1, 0), move(column, -1, 0)
    far, *extra = together(move(column, 2, 0), *extra)
    return jnp.concatenate([column, up, down, far], axis=0), *extra


def second_axis_rows(wide, staged, *extra):
    half = wide.shape[0] // 2
    top, low = wide[:half], wide[half:]
    up_top, down_low = move(top, 1, 1), move(low, -1, 1)
    top, low, staged = together(top, low, staged)
    up_low, down_top = move(low, 1, 1), move(top, -1, 1)
    up_top, down_low, *extra = together(up_top, down_low, *extra)
    far_top, far_low = move(up_top, 1, 1), move(down_low, -1, 1)
    rows = jnp.concatenate([wide, up_top, up_low, down_top, down_low, far_top, far_low], axis=0)
    return rows, staged, *extra


def narrow(*values):
    return add(*values).astype(jnp.bfloat16)


def fold_second_axis(partial):
    rows = partial.shape[0] // 8
    own_top, own_low, up_top, up_low, down_top, down_low, far_top, far_low = (
        partial[i * rows : (i + 1) * rows] for i in range(8)
    )
    via_top, via_low = together(move(far_top, -1, 1), move(far_low, 1, 1))
    back_low, fore_top = move(up_low, -1, 1), move(down_top, 1, 1)
    back_top, fore_low = together(narrow(up_top, via_top), narrow(down_low, via_low))
    back_top, fore_low = move(back_top, -1, 1), move(fore_low, 1, 1)
    return jnp.concatenate(
        [narrow(own_top, back_top, fore_top), narrow(own_low, back_low, fore_low)], axis=0
    )


def fold_first_axis(partial):
    rows = partial.shape[0] // 4
    own, up, down, far = (partial[i * rows : (i + 1) * rows] for i in range(4))
    far = together(move(far, 2, 0))[0]
    return narrow(own, move(up, -1, 0), move(down, 1, 0), far)


def fold_column(partial):
    depth, width = lax.axis_size("z"), partial.shape[1]
    arrived = lax.all_to_all(partial.reshape(depth, 2, width), "z", 0, 0, tiled=True)
    return jnp.sum(arrived.astype(jnp.float32), axis=0)


def spread_kernel(target_ref, token_ref, route_ref, gate_ref, out_ref):
    depth, rows, width = out_ref.shape
    lane = lax.broadcasted_iota(jnp.int32, (rows, META), 1)
    row = lax.broadcasted_iota(jnp.int32, (rows, META), 0)
    routes = route_ref[...].astype(jnp.float32)
    gates = gate_ref[...].astype(jnp.float32)
    meta = jnp.zeros((rows, META), jnp.float32)
    for index in range(routes.shape[1]):
        meta = jnp.where(lane == index, routes[:, index : index + 1], meta)
        meta = jnp.where(lane == 8 + index, gates[:, index : index + 1], meta)
    goal = jnp.where(row == 0, target_ref[0], target_ref[1])
    meta = jnp.where(lane == 16, (goal >> 8).astype(jnp.float32), meta)
    meta = jnp.where(lane == 17, (goal & 255).astype(jnp.float32), meta)
    meta = meta.astype(jnp.bfloat16)
    for index in range(depth):
        out_ref[index, :, : width - META] = token_ref[...]
        out_ref[index, :, width - META :] = meta


def spread_tokens(tokens, routes, route_gates, targets, depth):
    rows, width = tokens.shape
    return pl.pallas_call(
        spread_kernel,
        out_shape=jax.ShapeDtypeStruct((depth, rows, width + META), tokens.dtype),
        in_specs=[SMEM, VMEM, VMEM, VMEM],
        out_specs=VMEM,
        name="spread",
    )(targets, tokens, routes, route_gates)


def stage_kernel(*refs):
    sources, out, sems = refs[:-2], refs[-2], refs[-1]
    rows = sources[0].shape[0]
    copies = [
        pltpu.make_async_copy(source, out.at[pl.ds(index * rows, rows)], sems.at[index])
        for index, source in enumerate(sources)
    ]
    for copy in copies:
        copy.start()
    for copy in copies:
        copy.wait()


def stage(*weights):
    rows, width = weights[0].shape
    shape = (len(weights) * rows, width)
    return pl.pallas_call(
        stage_kernel,
        out_shape=pltpu.VMEM(shape, weights[0].dtype),
        in_specs=[ANY] * len(weights),
        out_specs=VMEM,
        scratch_shapes=[pltpu.SemaphoreType.DMA((len(weights),))],
        cost_estimate=pl.CostEstimate(
            flops=0, bytes_accessed=4 * shape[0] * shape[1], transcendentals=0
        ),
        compiler_params=pltpu.CompilerParams(vmem_limit_bytes=2**20),
        name="stage",
    )(*weights)


def expert_kernel(expert_ref, row_ref, in_ref, down_ref, out_ref, meta_ref, inner, active):
    width, units = down_ref.shape[1], down_ref.shape[0]
    part = 256
    for start in range(0, 2 * units, part):
        inner[:, start : start + part] = lax.dot_general(
            row_ref[:, :width],
            in_ref[start : start + part, :],
            (((1,), (1,)), ((), ())),
            preferred_element_type=jnp.float32,
        )
    meta = row_ref[:, width:].astype(jnp.float32)
    meta_ref[...] = meta
    lane = lax.broadcasted_iota(jnp.int32, meta.shape, 1)
    gates = pltpu.roll(meta, META - 8, 1)
    chosen = (lane < 8) & (meta == expert_ref[0].astype(jnp.float32))
    share = jnp.sum(jnp.where(chosen, gates, 0.0), axis=1, keepdims=True)
    gate = inner[:, :units]
    value = gate / (1.0 + jnp.exp(-gate)) * inner[:, units:] * share
    active[...] = value.astype(jnp.bfloat16)
    step = width // 7

    @pl.loop(0, 7)
    def _(index):
        span = pl.ds(pl.multiple_of(index * step, step), step)
        out_ref[:, span] = jnp.dot(
            active[...], down_ref[:, span], preferred_element_type=jnp.float32
        ).astype(jnp.bfloat16)


def expert_layer(rows, in_weight, out_weight, expert):
    count = rows.shape[0]
    units, width = out_weight.shape
    return pl.pallas_call(
        expert_kernel,
        out_shape=[
            jax.ShapeDtypeStruct((count, width), jnp.bfloat16),
            jax.ShapeDtypeStruct((count, META), jnp.float32),
        ],
        in_specs=[SMEM, VMEM, VMEM, VMEM],
        out_specs=[VMEM, VMEM],
        scratch_shapes=[
            pltpu.VMEM((count, 2 * units), jnp.float32),
            pltpu.VMEM((count, units), jnp.bfloat16),
        ],
        cost_estimate=pl.CostEstimate(
            flops=6 * count * units * width,
            bytes_accessed=2 * (3 * units * width + 2 * count * width),
            transcendentals=count * units,
        ),
        compiler_params=pltpu.CompilerParams(vmem_limit_bytes=16 * 2**20),
        name="expert",
    )(expert, rows, in_weight, out_weight)


def stats_kernel(place_ref, own_ref, other_ref, meta_ref, *refs):
    out_ref, stats = refs[-2:]
    rows = own_ref.shape[0]
    lane = lax.broadcasted_iota(jnp.int32, (rows, META), 1)
    meta = meta_ref[...]
    goal = jnp.where(lane == 16, meta * 256.0, jnp.where(lane == 17, meta, 0.0))
    goal = jnp.sum(goal, axis=1, keepdims=True).astype(jnp.int32)
    own, other = own_ref[...], other_ref[...]
    top = jnp.maximum(jnp.max(own, axis=1, keepdims=True), jnp.max(other, axis=1, keepdims=True))
    total = jnp.zeros_like(top)
    picked = jnp.zeros_like(top)
    for which, value in enumerate((own, other)):
        total += jnp.sum(jnp.exp(value - top), axis=1, keepdims=True)
        column = lax.broadcasted_iota(jnp.int32, value.shape, 1) + place_ref[which]
        picked += jnp.sum(jnp.where(column == goal, value, 0.0), axis=1, keepdims=True)
    values = jnp.where(lane == 0, top, jnp.where(lane == 1, total, picked))
    stats[...] = jnp.where(lane < 3, values, 0.0)
    block = rows // 32
    for index in range(16):
        first = stats[pl.ds(index * 2 * block, block, 2), :]
        second = stats[pl.ds(index * 2 * block + 1, block, 2), :]
        target = pl.multiple_of(place_ref[2 + index] * block, block)
        out_ref[pl.ds(target, block), :] = first + pltpu.roll(second, 4, 1)


def combine_kernel(stats_ref, out_ref):
    stats = stats_ref[...]
    lane = lax.broadcasted_iota(jnp.int32, (1, META), 1)
    top = jnp.max(stats, axis=0, keepdims=True)
    scale = jnp.exp(stats - top)
    total = jnp.sum(pltpu.roll(scale, 1, 1) * stats, axis=0, keepdims=True)
    picked = jnp.sum(stats, axis=0, keepdims=True)
    result = pltpu.roll(picked, META - 2, 1) - top - jnp.log(pltpu.roll(total, META - 1, 1))
    for index in range(2):
        out_ref[index] = jnp.sum(jnp.where(lane == 4 * index, result, 0.0))


def combine(stats):
    return pl.pallas_call(
        combine_kernel,
        out_shape=jax.ShapeDtypeStruct((2,), jnp.float32),
        in_specs=[VMEM],
        out_specs=SMEM,
        compiler_params=pltpu.CompilerParams(vmem_limit_bytes=4 * 2**20),
        name="combine",
    )(stats)


def row_stats(own, other, meta, place, *signs):
    rows = own.shape[0]
    return pl.pallas_call(
        stats_kernel,
        out_shape=jax.ShapeDtypeStruct((rows // 2, META), jnp.float32),
        in_specs=[SMEM, VMEM, VMEM, VMEM] + [ANY] * len(signs),
        out_specs=VMEM,
        scratch_shapes=[pltpu.VMEM((rows, META), jnp.float32)],
        compiler_params=pltpu.CompilerParams(vmem_limit_bytes=8 * 2**20),
        name="row_stats",
    )(place, own, other, meta, *signs)


def shards(
    tokens,
    routes,
    route_gates,
    expert_gate,
    expert_up,
    expert_down,
    norm_gain,
    head_weight,
    targets,
):
    width, depth = tokens.shape[1], lax.axis_size("z")

    def product(left, right):
        return jnp.dot(left, right, preferred_element_type=jnp.float32)

    columns = head_weight.shape[1]
    core = lax.axis_index("c")
    chip = lax.axis_index(("x", "z", "y"))
    first = core == 0
    steps = jnp.array([0, -1, 1, 2], jnp.int32)
    outer, inner = steps[:, None], steps[None, :]
    from_x = (lax.axis_index("x") + jnp.where(first, inner, outer)) % lax.axis_size("x")
    from_y = (lax.axis_index("y") + jnp.where(first, outer, inner)) % lax.axis_size("y")
    place = jnp.concatenate(
        [
            ((chip * 2 + core) * columns)[None],
            ((chip * 2 + 1 - core) * columns)[None],
            (from_x * lax.axis_size("y") + from_y).reshape(16),
        ]
    ).astype(jnp.int32)
    expert = lax.axis_index(("x", "z")).astype(jnp.int32)[None]
    column, gate, up, place, expert = together(
        column_rows(spread_tokens(tokens, routes, route_gates, targets, depth)),
        swap(expert_gate),
        swap(expert_up),
        place,
        expert,
    )
    wide, down = first_axis_rows(column, swap(expert_down))
    rows, out_weight, gate, up, head = second_axis_rows(
        wide, stage(expert_down[0], down[0]), gate, up, swap(head_weight)
    )
    in_weight = stage(expert_gate[0].T, gate[0].T, expert_up[0].T, up[0].T)
    partial, meta = expert_layer(rows, in_weight, out_weight, expert)
    partial, first_sign = together(partial, swap(meta))
    folded = fold_second_axis(partial)
    moe = fold_column(fold_first_axis(folded))

    hidden = (tokens.astype(jnp.float32) + moe).astype(jnp.bfloat16)
    widened = hidden.astype(jnp.float32)
    inverse = lax.rsqrt(jnp.mean(widened * widened, axis=-1, keepdims=True) + 1e-06)
    normed = (widened * inverse * norm_gain).astype(jnp.bfloat16)

    column = column_rows(jnp.broadcast_to(normed[None], (depth,) + normed.shape))
    column, second_sign = together(column, swap(column))
    wide, head = first_axis_rows(column, head)
    every, head = second_axis_rows(wide, stage(head))
    stats = row_stats(product(every, head_weight), product(every, head), meta, place, first_sign, second_sign)
    arrived = lax.all_to_all(stats, ("x", "y", "z"), 0, 0, tiled=True)
    logprob = combine(arrived)
    return (logprob, hidden)


def solution(mesh):
    fine = Mesh(mesh.devices.reshape(4, 8, 4, 2), ("x", "z", "y", "c"))
    rows = ("x", "z", "y", "c")
    in_specs = (
        P(rows, None),
        P(rows, None),
        P(rows, None),
        P(("x", "z"), None, ("y", "c")),
        P(("x", "z"), None, ("y", "c")),
        P(("x", "z"), ("y", "c"), None),
        P(),
        P(None, rows),
        P(rows),
    )
    out_specs = (P(rows), P(rows, None))
    return jax.shard_map(shards, mesh=fine, in_specs=in_specs, out_specs=out_specs, check_vma=False)
```

```python
import jax
import jax.numpy as jnp
from jax import lax
from jax.experimental import pallas as pl
from jax.experimental.pallas import tpu as pltpu
from jax.sharding import Mesh, PartitionSpec as P

META = 128
PLANE = ("x", "y", "c")
ANY = pl.BlockSpec(memory_space=pl.ANY)
SMEM = pl.BlockSpec(memory_space=pltpu.SMEM)
VMEM = pl.BlockSpec(memory_space=pltpu.VMEM)


def move(value, step, along):
    nx, ny = lax.axis_size("x"), lax.axis_size("y")
    pairs = []
    for x in range(nx):
        for y in range(ny):
            for c in range(2):
                tx, ty = ((x + step) % nx, y) if c == along else (x, (y + step) % ny)
                pairs.append(((x * ny + y) * 2 + c, (tx * ny + ty) * 2 + c))
    return lax.ppermute(value, PLANE, pairs)


def swap(value):
    return lax.ppermute(value, "c", [(0, 1), (1, 0)])


def add(*values):
    total = values[0].astype(jnp.float32)
    for value in values[1:]:
        total = total + value.astype(jnp.float32)
    return total


def together(*values):
    return lax.optimization_barrier(values)


def column_rows(spread):
    depth, rows, width = spread.shape
    return lax.all_to_all(spread, "z", 0, 0, tiled=True).reshape(depth * rows, width)


def first_axis_rows(column, *extra):
    up, down = move(column, 1, 0), move(column, -1, 0)
    far, *extra = together(move(column, 2, 0), *extra)
    return jnp.concatenate([column, up, down, far], axis=0), *extra


def second_axis_rows(wide, staged, *extra):
    half = wide.shape[0] // 2
    top, low = wide[:half], wide[half:]
    up_top, down_low = move(top, 1, 1), move(low, -1, 1)
    top, low, staged = together(top, low, staged)
    up_low, down_top = move(low, 1, 1), move(top, -1, 1)
    up_top, down_low, *extra = together(up_top, down_low, *extra)
    far_top, far_low = move(up_top, 1, 1), move(down_low, -1, 1)
    rows = jnp.concatenate([wide, up_top, up_low, down_top, down_low, far_top, far_low], axis=0)
    return rows, staged, *extra


def narrow(*values):
    return add(*values).astype(jnp.bfloat16)


def fold_second_axis(partial):
    rows = partial.shape[0] // 8
    own_top, own_low, up_top, up_low, down_top, down_low, far_top, far_low = (
        partial[i * rows : (i + 1) * rows] for i in range(8)
    )
    via_top, via_low = together(move(far_top, -1, 1), move(far_low, 1, 1))
    back_low, fore_top = move(up_low, -1, 1), move(down_top, 1, 1)
    back_top, fore_low = together(narrow(up_top, via_top), narrow(down_low, via_low))
    back_top, fore_low = move(back_top, -1, 1), move(fore_low, 1, 1)
    return jnp.concatenate(
        [narrow(own_top, back_top, fore_top), narrow(own_low, back_low, fore_low)], axis=0
    )


def fold_first_axis(partial):
    rows = partial.shape[0] // 4
    own, up, down, far = (partial[i * rows : (i + 1) * rows] for i in range(4))
    far = together(move(far, 2, 0))[0]
    return narrow(own, move(up, -1, 0), move(down, 1, 0), far)


def fold_column(partial):
    depth, width = lax.axis_size("z"), partial.shape[1]
    arrived = lax.all_to_all(partial.reshape(depth, 2, width), "z", 0, 0, tiled=True)
    return jnp.sum(arrived.astype(jnp.float32), axis=0)


def spread_kernel(target_ref, token_ref, route_ref, gate_ref, out_ref):
    depth, rows, width = out_ref.shape
    lane = lax.broadcasted_iota(jnp.int32, (rows, META), 1)
    row = lax.broadcasted_iota(jnp.int32, (rows, META), 0)
    routes = route_ref[...].astype(jnp.float32)
    gates = gate_ref[...].astype(jnp.float32)
    meta = jnp.zeros((rows, META), jnp.float32)
    for index in range(routes.shape[1]):
        meta = jnp.where(lane == index, routes[:, index : index + 1], meta)
        meta = jnp.where(lane == 8 + index, gates[:, index : index + 1], meta)
    goal = jnp.where(row == 0, target_ref[0], target_ref[1])
    meta = jnp.where(lane == 16, (goal >> 8).astype(jnp.float32), meta)
    meta = jnp.where(lane == 17, (goal & 255).astype(jnp.float32), meta)
    meta = meta.astype(jnp.bfloat16)
    for index in range(depth):
        out_ref[index, :, : width - META] = token_ref[...]
        out_ref[index, :, width - META :] = meta


def spread_tokens(tokens, routes, route_gates, targets, depth):
    rows, width = tokens.shape
    return pl.pallas_call(
        spread_kernel,
        out_shape=jax.ShapeDtypeStruct((depth, rows, width + META), tokens.dtype),
        in_specs=[SMEM, VMEM, VMEM, VMEM],
        out_specs=VMEM,
        name="spread",
    )(targets, tokens, routes, route_gates)


def stage_kernel(*refs):
    sources, out, sems = refs[:-2], refs[-2], refs[-1]
    rows = sources[0].shape[0]
    copies = [
        pltpu.make_async_copy(source, out.at[pl.ds(index * rows, rows)], sems.at[index])
        for index, source in enumerate(sources)
    ]
    for copy in copies:
        copy.start()
    for copy in copies:
        copy.wait()


def stage(*weights):
    rows, width = weights[0].shape
    shape = (len(weights) * rows, width)
    return pl.pallas_call(
        stage_kernel,
        out_shape=pltpu.VMEM(shape, weights[0].dtype),
        in_specs=[ANY] * len(weights),
        out_specs=VMEM,
        scratch_shapes=[pltpu.SemaphoreType.DMA((len(weights),))],
        cost_estimate=pl.CostEstimate(
            flops=0, bytes_accessed=4 * shape[0] * shape[1], transcendentals=0
        ),
        compiler_params=pltpu.CompilerParams(vmem_limit_bytes=2**20),
        name="stage",
    )(*weights)


def expert_kernel(expert_ref, row_ref, in_ref, active_ref, meta_ref, inner):
    units, width = active_ref.shape[1], in_ref.shape[1]
    for start in range(0, 2 * units, 256):
        inner[:, start : start + 256] = lax.dot_general(
            row_ref[:, :width],
            in_ref[start : start + 256, :],
            (((1,), (1,)), ((), ())),
            preferred_element_type=jnp.float32,
        )
    meta = row_ref[:, width:].astype(jnp.float32)
    meta_ref[...] = meta
    lane = lax.broadcasted_iota(jnp.int32, meta.shape, 1)
    gates = pltpu.roll(meta, META - 8, 1)
    chosen = (lane < 8) & (meta == expert_ref[0].astype(jnp.float32))
    share = jnp.sum(jnp.where(chosen, gates, 0.0), axis=1, keepdims=True)
    gate = inner[:, :units]
    value = gate / (1.0 + jnp.exp(-gate)) * inner[:, units:] * share
    active_ref[...] = value.astype(jnp.bfloat16)


def expert_units(rows, in_weight, expert):
    count = rows.shape[0]
    units, width = in_weight.shape[0] // 2, in_weight.shape[1]
    return pl.pallas_call(
        expert_kernel,
        out_shape=[
            jax.ShapeDtypeStruct((count, units), jnp.bfloat16),
            jax.ShapeDtypeStruct((count, META), jnp.float32),
        ],
        in_specs=[SMEM, VMEM, VMEM],
        out_specs=[VMEM, VMEM],
        scratch_shapes=[pltpu.VMEM((count, 2 * units), jnp.float32)],
        cost_estimate=pl.CostEstimate(
            flops=4 * count * units * width,
            bytes_accessed=4 * units * width + 2 * count * width,
            transcendentals=count * units,
        ),
        compiler_params=pltpu.CompilerParams(vmem_limit_bytes=16 * 2**20),
        name="expert",
    )(expert, rows, in_weight)


def stats_kernel(place_ref, own_ref, other_ref, meta_ref, *refs):
    out_ref, stats = refs[-2:]
    rows = own_ref.shape[0]
    lane = lax.broadcasted_iota(jnp.int32, (rows, META), 1)
    meta = meta_ref[...]
    goal = jnp.where(lane == 16, meta * 256.0, jnp.where(lane == 17, meta, 0.0))
    goal = jnp.sum(goal, axis=1, keepdims=True).astype(jnp.int32)
    own, other = own_ref[...], other_ref[...]
    top = jnp.maximum(jnp.max(own, axis=1, keepdims=True), jnp.max(other, axis=1, keepdims=True))
    total = jnp.zeros_like(top)
    picked = jnp.zeros_like(top)
    for which, value in enumerate((own, other)):
        total += jnp.sum(jnp.exp(value - top), axis=1, keepdims=True)
        column = lax.broadcasted_iota(jnp.int32, value.shape, 1) + place_ref[which]
        picked += jnp.sum(jnp.where(column == goal, value, 0.0), axis=1, keepdims=True)
    values = jnp.where(lane == 0, top, jnp.where(lane == 1, total, picked))
    stats[...] = jnp.where(lane < 3, values, 0.0)
    block = rows // 32
    for index in range(16):
        first = stats[pl.ds(index * 2 * block, block, 2), :]
        second = stats[pl.ds(index * 2 * block + 1, block, 2), :]
        target = pl.multiple_of(place_ref[2 + index] * block, block)
        out_ref[pl.ds(target, block), :] = first + pltpu.roll(second, 4, 1)


def combine_kernel(stats_ref, out_ref):
    stats = stats_ref[...]
    lane = lax.broadcasted_iota(jnp.int32, (1, META), 1)
    top = jnp.max(stats, axis=0, keepdims=True)
    scale = jnp.exp(stats - top)
    total = jnp.sum(pltpu.roll(scale, 1, 1) * stats, axis=0, keepdims=True)
    picked = jnp.sum(stats, axis=0, keepdims=True)
    result = pltpu.roll(picked, META - 2, 1) - top - jnp.log(pltpu.roll(total, META - 1, 1))
    for index in range(2):
        out_ref[index] = jnp.sum(jnp.where(lane == 4 * index, result, 0.0))


def combine(stats):
    return pl.pallas_call(
        combine_kernel,
        out_shape=jax.ShapeDtypeStruct((2,), jnp.float32),
        in_specs=[VMEM],
        out_specs=SMEM,
        compiler_params=pltpu.CompilerParams(vmem_limit_bytes=4 * 2**20),
        name="combine",
    )(stats)


def row_stats(own, other, meta, place, *signs):
    rows = own.shape[0]
    return pl.pallas_call(
        stats_kernel,
        out_shape=jax.ShapeDtypeStruct((rows // 2, META), jnp.float32),
        in_specs=[SMEM, VMEM, VMEM, VMEM] + [ANY] * len(signs),
        out_specs=VMEM,
        scratch_shapes=[pltpu.VMEM((rows, META), jnp.float32)],
        compiler_params=pltpu.CompilerParams(vmem_limit_bytes=8 * 2**20),
        name="row_stats",
    )(place, own, other, meta, *signs)


def shards(
    tokens,
    routes,
    route_gates,
    expert_gate,
    expert_up,
    expert_down,
    norm_gain,
    head_weight,
    targets,
):
    width, depth = tokens.shape[1], lax.axis_size("z")

    def product(left, right):
        return jnp.dot(left, right, preferred_element_type=jnp.float32)

    columns = head_weight.shape[1]
    core = lax.axis_index("c")
    chip = lax.axis_index(("x", "z", "y"))
    first = core == 0
    steps = jnp.array([0, -1, 1, 2], jnp.int32)
    outer, inner = steps[:, None], steps[None, :]
    from_x = (lax.axis_index("x") + jnp.where(first, inner, outer)) % lax.axis_size("x")
    from_y = (lax.axis_index("y") + jnp.where(first, outer, inner)) % lax.axis_size("y")
    place = jnp.concatenate(
        [
            ((chip * 2 + core) * columns)[None],
            ((chip * 2 + 1 - core) * columns)[None],
            (from_x * lax.axis_size("y") + from_y).reshape(16),
        ]
    ).astype(jnp.int32)
    expert = lax.axis_index(("x", "z")).astype(jnp.int32)[None]
    column, gate, up, place, expert = together(
        column_rows(spread_tokens(tokens, routes, route_gates, targets, depth)),
        swap(expert_gate),
        swap(expert_up),
        place,
        expert,
    )
    wide, down = first_axis_rows(column, swap(expert_down))
    rows, out_weight, gate, up, head = second_axis_rows(
        wide, stage(expert_down[0], down[0]), gate, up, swap(head_weight)
    )
    in_weight = stage(expert_gate[0].T, gate[0].T, expert_up[0].T, up[0].T)
    active, meta = expert_units(rows, in_weight, expert)
    partial, first_sign = together(product(active, out_weight).astype(jnp.bfloat16), swap(meta))
    folded = fold_second_axis(partial)
    moe = fold_column(fold_first_axis(folded))

    hidden = (tokens.astype(jnp.float32) + moe).astype(jnp.bfloat16)
    widened = hidden.astype(jnp.float32)
    inverse = lax.rsqrt(jnp.mean(widened * widened, axis=-1, keepdims=True) + 1e-06)
    normed = (widened * inverse * norm_gain).astype(jnp.bfloat16)

    column = column_rows(jnp.broadcast_to(normed[None], (depth,) + normed.shape))
    column, second_sign = together(column, swap(column))
    wide, head = first_axis_rows(column, head)
    every, head = second_axis_rows(wide, stage(head))
    stats = row_stats(product(every, head_weight), product(every, head), meta, place, first_sign, second_sign)
    arrived = lax.all_to_all(stats, ("x", "y", "z"), 0, 0, tiled=True)
    logprob = combine(arrived)
    return (logprob, hidden)


def solution(mesh):
    fine = Mesh(mesh.devices.reshape(4, 8, 4, 2), ("x", "z", "y", "c"))
    rows = ("x", "z", "y", "c")
    in_specs = (
        P(rows, None),
        P(rows, None),
        P(rows, None),
        P(("x", "z"), None, ("y", "c")),
        P(("x", "z"), None, ("y", "c")),
        P(("x", "z"), ("y", "c"), None),
        P(),
        P(None, rows),
        P(rows),
    )
    out_specs = (P(rows), P(rows, None))
    return jax.shard_map(shards, mesh=fine, in_specs=in_specs, out_specs=out_specs, check_vma=False)
```

```python
import jax
import jax.numpy as jnp
from jax import lax
from jax.experimental import pallas as pl
from jax.experimental.pallas import tpu as pltpu
from jax.sharding import Mesh, PartitionSpec as P

META = 128
PLANE = ("x", "y", "c")
ANY = pl.BlockSpec(memory_space=pl.ANY)
SMEM = pl.BlockSpec(memory_space=pltpu.SMEM)
VMEM = pl.BlockSpec(memory_space=pltpu.VMEM)


def move(value, step, along):
    nx, ny = lax.axis_size("x"), lax.axis_size("y")
    pairs = []
    for x in range(nx):
        for y in range(ny):
            for c in range(2):
                tx, ty = ((x + step) % nx, y) if c == along else (x, (y + step) % ny)
                pairs.append(((x * ny + y) * 2 + c, (tx * ny + ty) * 2 + c))
    return lax.ppermute(value, PLANE, pairs)


def swap(value):
    return lax.ppermute(value, "c", [(0, 1), (1, 0)])


def add(*values):
    total = values[0].astype(jnp.float32)
    for value in values[1:]:
        total = total + value.astype(jnp.float32)
    return total


def together(*values):
    return lax.optimization_barrier(values)


def column_rows(spread):
    depth, rows, width = spread.shape
    return lax.all_to_all(spread, "z", 0, 0, tiled=True).reshape(depth * rows, width)


def first_axis_rows(column, *extra):
    up, down = move(column, 1, 0), move(column, -1, 0)
    far, *extra = together(move(column, 2, 0), *extra)
    return jnp.concatenate([column, up, down, far], axis=0), *extra


def second_axis_rows(wide, staged, *extra):
    half = wide.shape[0] // 2
    top, low = wide[:half], wide[half:]
    up_top, down_low = move(top, 1, 1), move(low, -1, 1)
    top, low, staged = together(top, low, staged)
    up_low, down_top = move(low, 1, 1), move(top, -1, 1)
    up_top, down_low, *extra = together(up_top, down_low, *extra)
    far_top, far_low = move(up_top, 1, 1), move(down_low, -1, 1)
    near = jnp.concatenate([wide, up_top, up_low, down_top, down_low], axis=0)
    return near, jnp.concatenate([far_top, far_low], axis=0), staged, *extra


def narrow(*values):
    return add(*values).astype(jnp.bfloat16)


def fold_second_axis(partial):
    rows = partial.shape[0] // 8
    own_top, own_low, up_top, up_low, down_top, down_low, far_top, far_low = (
        partial[i * rows : (i + 1) * rows] for i in range(8)
    )
    via_top, via_low = together(move(far_top, -1, 1), move(far_low, 1, 1))
    back_low, fore_top = move(up_low, -1, 1), move(down_top, 1, 1)
    back_top, fore_low = together(narrow(up_top, via_top), narrow(down_low, via_low))
    back_top, fore_low = move(back_top, -1, 1), move(fore_low, 1, 1)
    return jnp.concatenate(
        [narrow(own_top, back_top, fore_top), narrow(own_low, back_low, fore_low)], axis=0
    )


def fold_first_axis(partial):
    rows = partial.shape[0] // 4
    own, up, down, far = (partial[i * rows : (i + 1) * rows] for i in range(4))
    far = together(move(far, 2, 0))[0]
    return narrow(own, move(up, -1, 0), move(down, 1, 0), far)


def fold_column(partial):
    depth, width = lax.axis_size("z"), partial.shape[1]
    arrived = lax.all_to_all(partial.reshape(depth, 2, width), "z", 0, 0, tiled=True)
    return jnp.sum(arrived.astype(jnp.float32), axis=0)


def spread_kernel(target_ref, token_ref, route_ref, gate_ref, out_ref):
    depth, rows, width = out_ref.shape
    lane = lax.broadcasted_iota(jnp.int32, (rows, META), 1)
    row = lax.broadcasted_iota(jnp.int32, (rows, META), 0)
    routes = route_ref[...].astype(jnp.float32)
    gates = gate_ref[...].astype(jnp.float32)
    meta = jnp.zeros((rows, META), jnp.float32)
    for index in range(routes.shape[1]):
        meta = jnp.where(lane == index, routes[:, index : index + 1], meta)
        meta = jnp.where(lane == 8 + index, gates[:, index : index + 1], meta)
    goal = jnp.where(row == 0, target_ref[0], target_ref[1])
    meta = jnp.where(lane == 16, (goal >> 8).astype(jnp.float32), meta)
    meta = jnp.where(lane == 17, (goal & 255).astype(jnp.float32), meta)
    meta = meta.astype(jnp.bfloat16)
    for index in range(depth):
        out_ref[index, :, : width - META] = token_ref[...]
        out_ref[index, :, width - META :] = meta


def spread_tokens(tokens, routes, route_gates, targets, depth):
    rows, width = tokens.shape
    return pl.pallas_call(
        spread_kernel,
        out_shape=jax.ShapeDtypeStruct((depth, rows, width + META), tokens.dtype),
        in_specs=[SMEM, VMEM, VMEM, VMEM],
        out_specs=VMEM,
        name="spread",
    )(targets, tokens, routes, route_gates)


def stage_kernel(*refs):
    sources, out, sems = refs[:-2], refs[-2], refs[-1]
    rows = sources[0].shape[0]
    copies = [
        pltpu.make_async_copy(source, out.at[pl.ds(index * rows, rows)], sems.at[index])
        for index, source in enumerate(sources)
    ]
    for copy in copies:
        copy.start()
    for copy in copies:
        copy.wait()


def stage(*weights):
    rows, width = weights[0].shape
    shape = (len(weights) * rows, width)
    return pl.pallas_call(
        stage_kernel,
        out_shape=pltpu.VMEM(shape, weights[0].dtype),
        in_specs=[ANY] * len(weights),
        out_specs=VMEM,
        scratch_shapes=[pltpu.SemaphoreType.DMA((len(weights),))],
        cost_estimate=pl.CostEstimate(
            flops=0, bytes_accessed=4 * shape[0] * shape[1], transcendentals=0
        ),
        compiler_params=pltpu.CompilerParams(vmem_limit_bytes=2**20),
        name="stage",
    )(*weights)


def expert_kernel(expert_ref, row_ref, in_ref, active_ref, meta_ref, inner):
    units, width = active_ref.shape[1], in_ref.shape[1]
    for start in range(0, 2 * units, 256):
        inner[:, start : start + 256] = lax.dot_general(
            row_ref[:, :width],
            in_ref[start : start + 256, :],
            (((1,), (1,)), ((), ())),
            preferred_element_type=jnp.float32,
        )
    meta = row_ref[:, width:].astype(jnp.float32)
    meta_ref[...] = meta
    lane = lax.broadcasted_iota(jnp.int32, meta.shape, 1)
    gates = pltpu.roll(meta, META - 8, 1)
    chosen = (lane < 8) & (meta == expert_ref[0].astype(jnp.float32))
    share = jnp.sum(jnp.where(chosen, gates, 0.0), axis=1, keepdims=True)
    gate = inner[:, :units]
    value = gate / (1.0 + jnp.exp(-gate)) * inner[:, units:] * share
    active_ref[...] = value.astype(jnp.bfloat16)


def expert_units(rows, in_weight, expert):
    count = rows.shape[0]
    units, width = in_weight.shape[0] // 2, in_weight.shape[1]
    return pl.pallas_call(
        expert_kernel,
        out_shape=[
            jax.ShapeDtypeStruct((count, units), jnp.bfloat16),
            jax.ShapeDtypeStruct((count, META), jnp.float32),
        ],
        in_specs=[SMEM, VMEM, VMEM],
        out_specs=[VMEM, VMEM],
        scratch_shapes=[pltpu.VMEM((count, 2 * units), jnp.float32)],
        cost_estimate=pl.CostEstimate(
            flops=4 * count * units * width,
            bytes_accessed=4 * units * width + 2 * count * width,
            transcendentals=count * units,
        ),
        compiler_params=pltpu.CompilerParams(vmem_limit_bytes=16 * 2**20),
        name="expert",
    )(expert, rows, in_weight)


def stats_kernel(place_ref, near_own, near_other, far_own, far_other, meta_ref, *refs):
    out_ref, stats = refs[-2:]
    rows = meta_ref.shape[0]
    lane = lax.broadcasted_iota(jnp.int32, (rows, META), 1)
    meta = meta_ref[...]
    goal = jnp.where(lane == 16, meta * 256.0, jnp.where(lane == 17, meta, 0.0))
    goal = jnp.sum(goal, axis=1, keepdims=True).astype(jnp.int32)
    own = jnp.concatenate([near_own[...], far_own[...]], axis=0)
    other = jnp.concatenate([near_other[...], far_other[...]], axis=0)
    top = jnp.maximum(jnp.max(own, axis=1, keepdims=True), jnp.max(other, axis=1, keepdims=True))
    total = jnp.zeros_like(top)
    picked = jnp.zeros_like(top)
    for which, value in enumerate((own, other)):
        total += jnp.sum(jnp.exp(value - top), axis=1, keepdims=True)
        column = lax.broadcasted_iota(jnp.int32, value.shape, 1) + place_ref[which]
        picked += jnp.sum(jnp.where(column == goal, value, 0.0), axis=1, keepdims=True)
    values = jnp.where(lane == 0, top, jnp.where(lane == 1, total, picked))
    stats[...] = jnp.where(lane < 3, values, 0.0)
    block = rows // 32
    for index in range(16):
        first = stats[pl.ds(index * 2 * block, block, 2), :]
        second = stats[pl.ds(index * 2 * block + 1, block, 2), :]
        target = pl.multiple_of(place_ref[2 + index] * block, block)
        out_ref[pl.ds(target, block), :] = first + pltpu.roll(second, 4, 1)


def combine_kernel(stats_ref, out_ref):
    stats = stats_ref[...]
    lane = lax.broadcasted_iota(jnp.int32, (1, META), 1)
    top = jnp.max(stats, axis=0, keepdims=True)
    scale = jnp.exp(stats - top)
    total = jnp.sum(pltpu.roll(scale, 1, 1) * stats, axis=0, keepdims=True)
    picked = jnp.sum(stats, axis=0, keepdims=True)
    result = pltpu.roll(picked, META - 2, 1) - top - jnp.log(pltpu.roll(total, META - 1, 1))
    for index in range(2):
        out_ref[index] = jnp.sum(jnp.where(lane == 4 * index, result, 0.0))


def combine(stats):
    return pl.pallas_call(
        combine_kernel,
        out_shape=jax.ShapeDtypeStruct((2,), jnp.float32),
        in_specs=[VMEM],
        out_specs=SMEM,
        compiler_params=pltpu.CompilerParams(vmem_limit_bytes=4 * 2**20),
        name="combine",
    )(stats)


def row_stats(near, far, meta, place, *signs):
    rows = meta.shape[0]
    return pl.pallas_call(
        stats_kernel,
        out_shape=jax.ShapeDtypeStruct((rows // 2, META), jnp.float32),
        in_specs=[SMEM] + [VMEM] * 5 + [ANY] * len(signs),
        out_specs=VMEM,
        scratch_shapes=[pltpu.VMEM((rows, META), jnp.float32)],
        compiler_params=pltpu.CompilerParams(vmem_limit_bytes=8 * 2**20),
        name="row_stats",
    )(place, *near, *far, meta, *signs)


def shards(
    tokens,
    routes,
    route_gates,
    expert_gate,
    expert_up,
    expert_down,
    norm_gain,
    head_weight,
    targets,
):
    width, depth = tokens.shape[1], lax.axis_size("z")

    def product(left, right):
        return jnp.dot(left, right, preferred_element_type=jnp.float32)

    columns = head_weight.shape[1]
    core = lax.axis_index("c")
    chip = lax.axis_index(("x", "z", "y"))
    first = core == 0
    steps = jnp.array([0, -1, 1, 2], jnp.int32)
    outer, inner = steps[:, None], steps[None, :]
    from_x = (lax.axis_index("x") + jnp.where(first, inner, outer)) % lax.axis_size("x")
    from_y = (lax.axis_index("y") + jnp.where(first, outer, inner)) % lax.axis_size("y")
    place = jnp.concatenate(
        [
            ((chip * 2 + core) * columns)[None],
            ((chip * 2 + 1 - core) * columns)[None],
            (from_x * lax.axis_size("y") + from_y).reshape(16),
        ]
    ).astype(jnp.int32)
    expert = lax.axis_index(("x", "z")).astype(jnp.int32)[None]
    column, gate, up, place, expert = together(
        column_rows(spread_tokens(tokens, routes, route_gates, targets, depth)),
        swap(expert_gate),
        swap(expert_up),
        place,
        expert,
    )
    wide, down = first_axis_rows(column, swap(expert_down))
    near, far, out_weight, gate, up, head = second_axis_rows(
        wide, stage(expert_down[0], down[0]), gate, up, swap(head_weight)
    )
    rows = jnp.concatenate([near, far], axis=0)
    in_weight = stage(expert_gate[0].T, gate[0].T, expert_up[0].T, up[0].T)
    active, meta = expert_units(rows, in_weight, expert)
    partial, first_sign = together(product(active, out_weight).astype(jnp.bfloat16), swap(meta))
    folded = fold_second_axis(partial)
    moe = fold_column(fold_first_axis(folded))

    hidden = (tokens.astype(jnp.float32) + moe).astype(jnp.bfloat16)
    widened = hidden.astype(jnp.float32)
    inverse = lax.rsqrt(jnp.mean(widened * widened, axis=-1, keepdims=True) + 1e-06)
    normed = (widened * inverse * norm_gain).astype(jnp.bfloat16)

    column = column_rows(jnp.broadcast_to(normed[None], (depth,) + normed.shape))
    column, second_sign = together(column, swap(column))
    wide, head = first_axis_rows(column, head)
    near, far, head = second_axis_rows(wide, stage(head))
    logits = [[product(part, weight) for weight in (head_weight, head)] for part in (near, far)]
    stats = row_stats(*logits, meta, place, first_sign, second_sign)
    arrived = lax.all_to_all(stats, ("x", "y", "z"), 0, 0, tiled=True)
    logprob = combine(arrived)
    return (logprob, hidden)


def solution(mesh):
    fine = Mesh(mesh.devices.reshape(4, 8, 4, 2), ("x", "z", "y", "c"))
    rows = ("x", "z", "y", "c")
    in_specs = (
        P(rows, None),
        P(rows, None),
        P(rows, None),
        P(("x", "z"), None, ("y", "c")),
        P(("x", "z"), None, ("y", "c")),
        P(("x", "z"), ("y", "c"), None),
        P(),
        P(None, rows),
        P(rows),
    )
    out_specs = (P(rows), P(rows, None))
    return jax.shard_map(shards, mesh=fine, in_specs=in_specs, out_specs=out_specs, check_vma=False)
```

```python
import jax
import jax.numpy as jnp
from jax import lax
from jax.experimental import pallas as pl
from jax.experimental.pallas import tpu as pltpu
from jax.sharding import Mesh, PartitionSpec as P

META = 128
PLANE = ("x", "y", "c")
ANY = pl.BlockSpec(memory_space=pl.ANY)
SMEM = pl.BlockSpec(memory_space=pltpu.SMEM)
VMEM = pl.BlockSpec(memory_space=pltpu.VMEM)


def move(value, step, along):
    nx, ny = lax.axis_size("x"), lax.axis_size("y")
    pairs = []
    for x in range(nx):
        for y in range(ny):
            for c in range(2):
                tx, ty = ((x + step) % nx, y) if c == along else (x, (y + step) % ny)
                pairs.append(((x * ny + y) * 2 + c, (tx * ny + ty) * 2 + c))
    return lax.ppermute(value, PLANE, pairs)


def swap(value):
    return lax.ppermute(value, "c", [(0, 1), (1, 0)])


def add(*values):
    total = values[0].astype(jnp.float32)
    for value in values[1:]:
        total = total + value.astype(jnp.float32)
    return total


def together(*values):
    return lax.optimization_barrier(values)


def column_rows(spread):
    depth, rows, width = spread.shape
    return lax.all_to_all(spread, "z", 0, 0, tiled=True).reshape(depth * rows, width)


def first_axis_rows(column, *extra):
    up, down = move(column, 1, 0), move(column, -1, 0)
    far, *extra = together(move(column, 2, 0), *extra)
    return jnp.concatenate([column, up, down, far], axis=0), *extra


def second_axis_rows(wide, staged, *extra):
    half = wide.shape[0] // 2
    top, low = wide[:half], wide[half:]
    up_top, down_low = move(top, 1, 1), move(low, -1, 1)
    top, low, staged = together(top, low, staged)
    up_low, down_top = move(low, 1, 1), move(top, -1, 1)
    up_top, down_low, *extra = together(up_top, down_low, *extra)
    far_top, far_low = move(up_top, 1, 1), move(down_low, -1, 1)
    near = jnp.concatenate([wide, up_top, up_low, down_top, down_low], axis=0)
    return near, jnp.concatenate([far_top, far_low], axis=0), staged, *extra


def narrow(*values):
    return add(*values).astype(jnp.bfloat16)


def fold_second_axis(partial):
    rows = partial.shape[0] // 8
    own_top, own_low, up_top, up_low, down_top, down_low, far_top, far_low = (
        partial[i * rows : (i + 1) * rows] for i in range(8)
    )
    via_top, via_low = together(move(far_top, -1, 1), move(far_low, 1, 1))
    back_low, fore_top = move(up_low, -1, 1), move(down_top, 1, 1)
    back_top, fore_low = together(narrow(up_top, via_top), narrow(down_low, via_low))
    back_top, fore_low = move(back_top, -1, 1), move(fore_low, 1, 1)
    return jnp.concatenate(
        [narrow(own_top, back_top, fore_top), narrow(own_low, back_low, fore_low)], axis=0
    )


def fold_first_axis(partial):
    rows = partial.shape[0] // 4
    own, up, down, far = (partial[i * rows : (i + 1) * rows] for i in range(4))
    far = together(move(far, 2, 0))[0]
    return narrow(own, move(up, -1, 0), move(down, 1, 0), far)


def fold_column(partial):
    depth, width = lax.axis_size("z"), partial.shape[1]
    arrived = lax.all_to_all(partial.reshape(depth, 2, width), "z", 0, 0, tiled=True)
    return jnp.sum(arrived.astype(jnp.float32), axis=0)


def spread_kernel(target_ref, token_ref, route_ref, gate_ref, out_ref):
    depth, rows, width = out_ref.shape
    lane = lax.broadcasted_iota(jnp.int32, (rows, META), 1)
    row = lax.broadcasted_iota(jnp.int32, (rows, META), 0)
    routes = route_ref[...].astype(jnp.float32)
    gates = gate_ref[...].astype(jnp.float32)
    meta = jnp.zeros((rows, META), jnp.float32)
    for index in range(routes.shape[1]):
        meta = jnp.where(lane == index, routes[:, index : index + 1], meta)
        meta = jnp.where(lane == 8 + index, gates[:, index : index + 1], meta)
    goal = jnp.where(row == 0, target_ref[0], target_ref[1])
    meta = jnp.where(lane == 16, (goal >> 8).astype(jnp.float32), meta)
    meta = jnp.where(lane == 17, (goal & 255).astype(jnp.float32), meta)
    meta = meta.astype(jnp.bfloat16)
    for index in range(depth):
        out_ref[index, :, : width - META] = token_ref[...]
        out_ref[index, :, width - META :] = meta


def spread_tokens(tokens, routes, route_gates, targets, depth):
    rows, width = tokens.shape
    return pl.pallas_call(
        spread_kernel,
        out_shape=jax.ShapeDtypeStruct((depth, rows, width + META), tokens.dtype),
        in_specs=[SMEM, VMEM, VMEM, VMEM],
        out_specs=VMEM,
        name="spread",
    )(targets, tokens, routes, route_gates)


def stage_kernel(*refs):
    sources, out, sems = refs[:-2], refs[-2], refs[-1]
    rows = sources[0].shape[0]
    copies = [
        pltpu.make_async_copy(source, out.at[pl.ds(index * rows, rows)], sems.at[index])
        for index, source in enumerate(sources)
    ]
    for copy in copies:
        copy.start()
    for copy in copies:
        copy.wait()


def stage(*weights):
    rows, width = weights[0].shape
    shape = (len(weights) * rows, width)
    return pl.pallas_call(
        stage_kernel,
        out_shape=pltpu.VMEM(shape, weights[0].dtype),
        in_specs=[ANY] * len(weights),
        out_specs=VMEM,
        scratch_shapes=[pltpu.SemaphoreType.DMA((len(weights),))],
        cost_estimate=pl.CostEstimate(
            flops=0, bytes_accessed=4 * shape[0] * shape[1], transcendentals=0
        ),
        compiler_params=pltpu.CompilerParams(vmem_limit_bytes=2**20),
        name="stage",
    )(*weights)


def expert_kernel(expert_ref, row_ref, in_ref, active_ref, meta_ref, inner):
    units, width = active_ref.shape[1], in_ref.shape[1]
    for start in range(0, 2 * units, 256):
        inner[:, start : start + 256] = lax.dot_general(
            row_ref[:, :width],
            in_ref[start : start + 256, :],
            (((1,), (1,)), ((), ())),
            preferred_element_type=jnp.float32,
        )
    meta = row_ref[:, width:].astype(jnp.float32)
    meta_ref[...] = meta
    lane = lax.broadcasted_iota(jnp.int32, meta.shape, 1)
    gates = pltpu.roll(meta, META - 8, 1)
    chosen = (lane < 8) & (meta == expert_ref[0].astype(jnp.float32))
    share = jnp.sum(jnp.where(chosen, gates, 0.0), axis=1, keepdims=True)
    gate = inner[:, :units]
    value = gate / (1.0 + jnp.exp(-gate)) * inner[:, units:] * share
    active_ref[...] = value.astype(jnp.bfloat16)


def expert_units(rows, in_weight, expert):
    count = rows.shape[0]
    units, width = in_weight.shape[0] // 2, in_weight.shape[1]
    return pl.pallas_call(
        expert_kernel,
        out_shape=[
            jax.ShapeDtypeStruct((count, units), jnp.bfloat16),
            jax.ShapeDtypeStruct((count, META), jnp.float32),
        ],
        in_specs=[SMEM, VMEM, VMEM],
        out_specs=[VMEM, VMEM],
        scratch_shapes=[pltpu.VMEM((count, 2 * units), jnp.float32)],
        cost_estimate=pl.CostEstimate(
            flops=4 * count * units * width,
            bytes_accessed=4 * units * width + 2 * count * width,
            transcendentals=count * units,
        ),
        compiler_params=pltpu.CompilerParams(vmem_limit_bytes=16 * 2**20),
        name="expert",
    )(expert, rows, in_weight)


def stats_kernel(place_ref, near_own, near_other, far_own, far_other, meta_ref, *refs):
    out_ref, stats = refs[-2:]
    rows = meta_ref.shape[0]
    lane = lax.broadcasted_iota(jnp.int32, (rows, META), 1)
    meta = meta_ref[...]
    goal = jnp.where(lane == 16, meta * 256.0, jnp.where(lane == 17, meta, 0.0))
    goal = jnp.sum(goal, axis=1, keepdims=True).astype(jnp.int32)
    own = jnp.concatenate([near_own[...], far_own[...]], axis=0)
    other = jnp.concatenate([near_other[...], far_other[...]], axis=0)
    top = jnp.maximum(jnp.max(own, axis=1, keepdims=True), jnp.max(other, axis=1, keepdims=True))
    total = jnp.zeros_like(top)
    picked = jnp.zeros_like(top)
    for which, value in enumerate((own, other)):
        total += jnp.sum(jnp.exp(value - top), axis=1, keepdims=True)
        column = lax.broadcasted_iota(jnp.int32, value.shape, 1) + place_ref[which]
        picked += jnp.sum(jnp.where(column == goal, value, 0.0), axis=1, keepdims=True)
    values = jnp.where(lane == 0, top, jnp.where(lane == 1, total, picked))
    stats[...] = jnp.where(lane < 3, values, 0.0)
    block = rows // 32
    for index in range(16):
        first = stats[pl.ds(index * 2 * block, block, 2), :]
        second = stats[pl.ds(index * 2 * block + 1, block, 2), :]
        target = pl.multiple_of(place_ref[2 + index] * block, block)
        out_ref[pl.ds(target, block), :] = first + pltpu.roll(second, 4, 1)


def combine_kernel(stats_ref, out_ref):
    stats = stats_ref[...]
    lane = lax.broadcasted_iota(jnp.int32, (1, META), 1)
    top = jnp.max(stats, axis=0, keepdims=True)
    scale = jnp.exp(stats - top)
    total = jnp.sum(pltpu.roll(scale, 1, 1) * stats, axis=0, keepdims=True)
    picked = jnp.sum(stats, axis=0, keepdims=True)
    result = pltpu.roll(picked, META - 2, 1) - top - jnp.log(pltpu.roll(total, META - 1, 1))
    for index in range(2):
        out_ref[index] = jnp.sum(jnp.where(lane == 4 * index, result, 0.0))


def combine(stats):
    return pl.pallas_call(
        combine_kernel,
        out_shape=jax.ShapeDtypeStruct((2,), jnp.float32),
        in_specs=[VMEM],
        out_specs=SMEM,
        compiler_params=pltpu.CompilerParams(vmem_limit_bytes=4 * 2**20),
        name="combine",
    )(stats)


def row_stats(near, far, meta, place, *signs):
    rows = meta.shape[0]
    return pl.pallas_call(
        stats_kernel,
        out_shape=jax.ShapeDtypeStruct((rows // 2, META), jnp.float32),
        in_specs=[SMEM] + [VMEM] * 5 + [ANY] * len(signs),
        out_specs=VMEM,
        scratch_shapes=[pltpu.VMEM((rows, META), jnp.float32)],
        compiler_params=pltpu.CompilerParams(vmem_limit_bytes=8 * 2**20),
        name="row_stats",
    )(place, *near, *far, meta, *signs)


def shards(
    tokens,
    routes,
    route_gates,
    expert_gate,
    expert_up,
    expert_down,
    norm_gain,
    head_weight,
    targets,
):
    width, depth = tokens.shape[1], lax.axis_size("z")

    def product(left, right):
        return jnp.dot(left, right, preferred_element_type=jnp.float32)

    columns = head_weight.shape[1]
    core = lax.axis_index("c")
    chip = lax.axis_index(("x", "z", "y"))
    first = core == 0
    steps = jnp.array([0, -1, 1, 2], jnp.int32)
    outer, inner = steps[:, None], steps[None, :]
    from_x = (lax.axis_index("x") + jnp.where(first, inner, outer)) % lax.axis_size("x")
    from_y = (lax.axis_index("y") + jnp.where(first, outer, inner)) % lax.axis_size("y")
    place = jnp.concatenate(
        [
            ((chip * 2 + core) * columns)[None],
            ((chip * 2 + 1 - core) * columns)[None],
            (from_x * lax.axis_size("y") + from_y).reshape(16),
        ]
    ).astype(jnp.int32)
    expert = lax.axis_index(("x", "z")).astype(jnp.int32)[None]
    column, gate, up, place, expert = together(
        column_rows(spread_tokens(tokens, routes, route_gates, targets, depth)),
        swap(expert_gate),
        swap(expert_up),
        place,
        expert,
    )
    wide, down = first_axis_rows(column, swap(expert_down))
    near, far, out_weight, gate, up, head = second_axis_rows(
        wide, stage(expert_down[0], down[0]), gate, up, swap(head_weight)
    )
    rows = jnp.concatenate([near, far], axis=0)
    in_weight = stage(expert_gate[0].T, gate[0].T, expert_up[0].T, up[0].T)
    active, meta = expert_units(rows, in_weight, expert)
    partial, first_sign = together(product(active, out_weight).astype(jnp.bfloat16), swap(meta))
    folded = fold_second_axis(partial)
    moe = fold_column(fold_first_axis(folded))

    hidden = (tokens.astype(jnp.float32) + moe).astype(jnp.bfloat16)
    widened = hidden.astype(jnp.float32)
    inverse = lax.rsqrt(jnp.mean(widened * widened, axis=-1, keepdims=True) + 1e-06)
    normed = (widened * inverse * norm_gain).astype(jnp.bfloat16)

    column = column_rows(jnp.broadcast_to(normed[None], (depth,) + normed.shape))
    column, second_sign = together(column, swap(column[:, :META]))
    wide, head = first_axis_rows(column, head)
    near, far, head = second_axis_rows(wide, stage(head))
    logits = [[product(part, weight) for weight in (head_weight, head)] for part in (near, far)]
    stats = row_stats(*logits, meta, place, first_sign, second_sign)
    arrived = lax.all_to_all(stats, ("x", "y", "z"), 0, 0, tiled=True)
    logprob = combine(arrived)
    return (logprob, hidden)


def solution(mesh):
    fine = Mesh(mesh.devices.reshape(4, 8, 4, 2), ("x", "z", "y", "c"))
    rows = ("x", "z", "y", "c")
    in_specs = (
        P(rows, None),
        P(rows, None),
        P(rows, None),
        P(("x", "z"), None, ("y", "c")),
        P(("x", "z"), None, ("y", "c")),
        P(("x", "z"), ("y", "c"), None),
        P(),
        P(None, rows),
        P(rows),
    )
    out_specs = (P(rows), P(rows, None))
    return jax.shard_map(shards, mesh=fine, in_specs=in_specs, out_specs=out_specs, check_vma=False)
```
